32 devices in a mesh: groups: 2 (over y), tile: 4 (over x, core), cuts: 4 (over z).
Axes of the slice: x: 2, y: 2, z: 4, core: 2. Of those that a mesh axis runs over, the one named last changes fastest.
Arguments:
- trade: bfloat16 [16, 4, 256, 8192], P(('groups', 'cuts'), 'tile'), parts along dimension 0, may hold values from -6 to 6
- factor: bfloat16 [32768, 256], P(('groups', 'tile', 'cuts')), parts along dimension 0, may hold values from -0.375 to 0.375
- scales: float32 [16, 256], P(('groups', 'cuts')), parts along dimension 0, may hold values from 0.1 to 1.9
- core: float32 [512, 256], P('groups'), parts along dimension 0, may hold values from -4 to 4
Outputs:
- grad_factor: float32 [32768, 256], P(('groups', 'tile', 'cuts')), parts along dimension 0
- grad_window: float32 [1024, 256], P(('groups', 'cuts')), parts along dimension 0
- grad_core: float32 [512, 256], P('groups'), parts along dimension 0
- grad_scales: float32 [16, 256], P(('groups', 'cuts')), parts along dimension 0
The draws below stay inside these ranges and needn't reach their ends.
There are 2 independent parts, one for each index of `groups`. The reference program is written for one: setup_inputs(seed, part) draws one part's arguments, and reference() takes and returns one part's arrays. A program takes and returns all parts, laid end to end along the dimension named above; each array names one. Nothing has to cross between parts.
All inputs are finite; a program needn't handle non-finite values.
Results may differ from the reference program's by a relative error of at most 0.00055.
Values may be sent and summed in bfloat16 or wider, within the bound.
A program may use at most 128 MiB of HBM per device.

```python
import math
import jax
import jax.numpy as jnp
from jax import lax

N = 16384
P_SIZE = 256
TR = 2
ROWS_DEV = 256
K = 8
W = 512
COLS_DEV = 8192
N_TILE = 4


def with_spikes(drawn, key, source, target, parts, factor):
    def block_of(axis_at):
        return (jnp.arange(drawn.shape[axis_at]) // (drawn.shape[axis_at] // parts)).reshape((-1,) + (1,) * (drawn.ndim - 1 - axis_at))

    one_side = jax.random.permutation(key, parts)[block_of(target)]
    other_side = (block_of(target) + parts // 2) % parts
    return jnp.where((block_of(source) == one_side) | (block_of(source) == other_side), factor * drawn, drawn)


def shard_levels(rng, extent, cuts, low, high):
    gain = 1.0
    for dim, shards_of in cuts:
        steps = jax.random.uniform(jax.random.fold_in(jax.random.fold_in(rng, 6), dim), (shards_of,), jnp.float32, low / len(cuts), high / len(cuts))
        gain = gain * jnp.repeat(jnp.exp(steps), extent[dim] // shards_of).reshape((-1,) + (1,) * (len(extent) - 1 - dim))
    return gain


def noise(rng, dims, scale, bound, shards=(), held_as=jnp.bfloat16):
    entries = jax.random.normal(rng, dims, jnp.float32) * scale
    if len(shards) > 0:
        entries = shard_levels(rng, dims, shards, -0.22, 0.18) * entries
    return jnp.clip(entries, min=-bound, max=bound).astype(held_as)


def gaussian_with(own_key, extent, spread, limit, split, heavy, held_as=jnp.bfloat16):
    values = spread * jax.random.normal(own_key, extent, jnp.float32)
    if split:
        values = values * shard_levels(own_key, extent, split, -0.22, 0.18)
    return jnp.clip(with_spikes(values, jax.random.fold_in(own_key, 3), *heavy), -limit, limit).astype(held_as)


def setup_inputs(seed: int = 0, part: int = 0) -> dict:
    arg_keys = jax.random.split(jax.random.key(seed), 5)
    part_keys = jax.random.split(jax.random.fold_in(arg_keys[4], part), 5)
    return {
        "trade": gaussian_with(part_keys[0], (K, N_TILE, ROWS_DEV, COLS_DEV), 1.0, 6.0, ((0, 4), (1, 4)), (0, 3, 4, 2.0)),
        "factor": noise(part_keys[1], (N, P_SIZE), P_SIZE ** -0.5, 0.375, ((0, 16),)),
        "scales": jnp.clip(1.0 + 0.18 * jax.random.normal(part_keys[2], (K, P_SIZE), jnp.float32), 0.1, 1.9),
        "core": noise(part_keys[3], (P_SIZE, P_SIZE), 1.0, 4.0, (), jnp.float32),
    }


def reference(trade, factor, scales, core):
    bands = N_TILE // TR
    rows_band = ROWS_DEV
    cols_band = N // bands
    window32 = factor[:W].astype(jnp.float32)
    coef = 1.0 / math.sqrt(K * W)
    highest = lax.Precision.HIGHEST

    def one_month(carry, inputs):
        acc_factor, acc_window, acc_core = carry
        tiles, diag_k = inputs
        matrix = tiles.reshape(bands, TR, rows_band, cols_band).transpose(1, 2, 0, 3).reshape(W, N)
        inner = diag_k[:, None] * core * diag_k[None, :]
        mapped = jnp.dot(window32, inner, precision=highest).astype(jnp.bfloat16)
        model = jnp.dot(mapped, factor.T, preferred_element_type=jnp.float32)
        residual = (matrix.astype(jnp.float32) - model).astype(jnp.bfloat16)
        acc_factor = acc_factor + jnp.dot(residual.T, mapped, preferred_element_type=jnp.float32)
        projected = jnp.dot(residual, factor, preferred_element_type=jnp.float32)
        acc_window = acc_window + jnp.dot(projected, inner.T, precision=highest)
        gram = jnp.dot(window32.T, projected, precision=highest)
        acc_core = acc_core + diag_k[:, None] * gram * diag_k[None, :]
        weighted = gram * core
        grad_diag = jnp.dot(weighted, diag_k, precision=highest) + jnp.dot(weighted.T, diag_k, precision=highest)
        return ((acc_factor, acc_window, acc_core), grad_diag)
    start = (jnp.zeros((N, P_SIZE), jnp.float32), jnp.zeros((W, P_SIZE), jnp.float32), jnp.zeros((P_SIZE, P_SIZE), jnp.float32))
    (acc_factor, acc_window, acc_core), grad_diags = lax.scan(one_month, start, (trade, scales))
    return (-coef * acc_factor, -coef * acc_window, -coef * acc_core, -coef * grad_diags)
```

```python
import functools
import math

import jax
import jax.numpy as jnp
from jax import lax
from jax.experimental import pallas as pl
from jax.experimental.pallas import tpu as pltpu
from jax.sharding import PartitionSpec as P

HIGHEST = lax.Precision.HIGHEST
MESH = pl.DeviceIdType.MESH


def kernel(n, tiles, coef, trade, factor, scales, core, grad_ref, small_ref,
           tv, fac, win, acc, rbuf, fmat, bmat, bmat_t,
           tl_sem, ts_sem, tr_sem, own_sem, ag_send, ag_recv, rs_send, rs_recv, win_send, win_recv):
    z = lax.axis_index("cuts")
    t = lax.axis_index("tile")
    c = lax.rem(t, 2)
    partner = t + 1 - 2 * c
    months = trade.shape[0]
    rows = trade.shape[2]
    n_q, r = fac.shape[1], fac.shape[2]
    shard = n_q * r
    block = n * shard
    wsize = win.shape[0]
    pieces = win_recv.shape[0]
    wrow = wsize // pieces

    barrier = pltpu.get_barrier_semaphore()

    @pl.when(z > 0)
    def _():
        pl.semaphore_signal(barrier, inc=1, device_id={"cuts": z - 1}, device_id_type=MESH)

    @pl.when(z < n - 1)
    def _():
        pl.semaphore_signal(barrier, inc=1, device_id={"cuts": z + 1}, device_id_type=MESH)

    for k in range(1, tiles):
        pl.semaphore_signal(
            barrier, inc=1, device_id={"tile": lax.rem(t + k, tiles)}, device_id_type=MESH)

    def own_copy(q):
        return pltpu.make_async_copy(factor.at[pl.ds(q * r, r)], fac.at[z, q], own_sem.at[q])

    def local_trade(j, q):
        off = pl.multiple_of(c * block + j * shard + q * r, 128)
        return pltpu.make_async_copy(
            trade.at[:, 0, :, pl.ds(off, r)], tv.at[j, q, :, c], tl_sem.at[j, q])

    def remote_trade(j, q):
        off = pl.multiple_of((1 - c) * block + j * shard + q * r, 128)
        return pltpu.make_async_remote_copy(
            src_ref=trade.at[:, 0, :, pl.ds(off, r)], dst_ref=tv.at[j, q, :, c],
            send_sem=ts_sem.at[j, q], recv_sem=tr_sem.at[j, q],
            device_id={"tile": partner}, device_id_type=MESH)

    def recv_trade(j, q):
        off = pl.multiple_of(c * block + j * shard + q * r, 128)
        return pltpu.make_async_remote_copy(
            src_ref=trade.at[:, 0, :, pl.ds(off, r)], dst_ref=tv.at[j, q, :, 1 - c],
            send_sem=ts_sem.at[j, q], recv_sem=tr_sem.at[j, q],
            device_id={"tile": partner}, device_id_type=MESH)

    for q in range(n_q):
        own_copy(q).start()

    pl.semaphore_wait(
        barrier, tiles - 1 + jnp.where(z > 0, 1, 0) + jnp.where(z < n - 1, 1, 0))
    for q in range(n_q):
        own_copy(q).wait()

    def win_up(p):
        return pltpu.make_async_remote_copy(
            src_ref=win.at[pl.ds(p * wrow, wrow)], dst_ref=win.at[pl.ds(p * wrow, wrow)],
            send_sem=win_send.at[p, 0], recv_sem=win_recv.at[p],
            device_id={"cuts": z + 1}, device_id_type=MESH)

    def win_side(p, k):
        return pltpu.make_async_remote_copy(
            src_ref=win.at[pl.ds(p * wrow, wrow)], dst_ref=win.at[pl.ds(p * wrow, wrow)],
            send_sem=win_send.at[p, k], recv_sem=win_recv.at[p],
            device_id={"tile": k}, device_id_type=MESH)

    def win_recv_wait(p):
        win_up(p).wait_recv()

    @pl.when((t == 0) & (z == 0))
    def _():
        for p in range(pieces):
            win[pl.ds(p * wrow, wrow), :] = fac[0, p]

    @pl.when((t == 0) & (z == 0))
    def _():
        for p in range(pieces):
            if n > 1:
                win_up(p).start()
            for k in range(1, tiles):
                win_side(p, k).start()

    def mirrored(d, x):
        return jnp.where(d == 0, x, n - 1 - x)

    def ag_copy(d, j, q):
        return pltpu.make_async_remote_copy(
            src_ref=fac.at[j, q], dst_ref=fac.at[j, q],
            send_sem=ag_send.at[d, j, q], recv_sem=ag_recv.at[j, q],
            device_id={"cuts": z + 1 - 2 * d}, device_id_type=MESH)

    def gather_step(s, q):
        def one(d, carry):
            zm = mirrored(d, z)
            jm = zm - s

            @pl.when(jm >= 0)
            def _():
                j = mirrored(d, jm)

                @pl.when(s > 0)
                def _():
                    ag_copy(d, j, q).wait_recv()

                @pl.when(zm < n - 1)
                def _():
                    ag_copy(d, j, q).start()
            return carry
        lax.fori_loop(0, 2, one, 0)

    def gather_first(q, carry):
        gather_step(0, q)
        return carry
    lax.fori_loop(0, n_q, gather_first, 0)

    def trade_start(i, carry):
        s, q = i // n_q, i % n_q
        for d in (0, 1):
            zm = mirrored(d, z)

            @pl.when((zm - s >= 0) & ((s > 0) | (d == 0)))
            def _():
                j = mirrored(d, zm - s)
                local_trade(j, q).start()
                remote_trade(j, q).start()
        return carry
    lax.fori_loop(0, n * n_q, trade_start, 0)

    @pl.when((t != 0) | (z != 0))
    def _():
        for p in range(pieces):
            win_recv_wait(p)

            @pl.when(t == 0)
            def _():
                @pl.when(z < n - 1)
                def _():
                    win_up(p).start()
                for k in range(1, tiles):
                    win_side(p, k).start()

    def inner_of(m):
        drow = jnp.broadcast_to(scales[m:m + 1, :], core.shape)
        return drow.T * core[...] * drow

    win32 = win[...].astype(jnp.float32)
    for m in range(months):
        mapped = jnp.dot(win32, inner_of(m), precision=HIGHEST,
                         preferred_element_type=jnp.float32)
        bmat[m] = mapped.astype(jnp.bfloat16)
        bmat_t[m] = mapped.T.astype(jnp.bfloat16)
        fmat[m] = jnp.zeros_like(fmat[m])

    def compute(j, q):
        local_trade(j, q).wait()
        recv_trade(j, q).wait_recv()
        a = fac[j, q]
        total = None
        for m in range(months):
            x = jnp.concatenate([tv[j, q, m, 0], tv[j, q, m, 1]], 0)
            model = lax.dot_general(bmat[m], a, (((1,), (1,)), ((), ())),
                                    preferred_element_type=jnp.float32)
            e = (x.astype(jnp.float32) - model).astype(jnp.bfloat16)
            term = jnp.dot(bmat_t[m], e, preferred_element_type=jnp.float32)
            total = term if total is None else total + term
            fmat[m] += jnp.dot(e, a, preferred_element_type=jnp.float32)
        acc[j, q] = total

    def compute_step(s, q):
        def one(d, carry):
            jm = mirrored(d, z) - s

            @pl.when((jm >= 0) & ((s > 0) | (d == 0)))
            def _():
                compute(mirrored(d, jm), q)
            return carry
        lax.fori_loop(0, 2, one, 0)

    def rs_copy(d, j, q):
        to = z + 1 - 2 * d
        slot = jnp.where((j == to) & (d == 1), n, j)
        return pltpu.make_async_remote_copy(
            src_ref=acc.at[j, q], dst_ref=rbuf.at[slot, q],
            send_sem=rs_send.at[j, q], recv_sem=rs_recv.at[slot, q],
            device_id={"cuts": to}, device_id_type=MESH)

    def rs_wait(d, slot, q):
        pltpu.make_async_remote_copy(
            src_ref=acc.at[0, q], dst_ref=rbuf.at[slot, q],
            send_sem=rs_send.at[0, q], recv_sem=rs_recv.at[slot, q],
            device_id={"cuts": z + 1 - 2 * d}, device_id_type=MESH).wait_recv()

    def reduce_step(s, q):
        def one(d, carry):
            zm = mirrored(d, z)
            jm = s - zm

            @pl.when((jm > zm) & (jm <= n - 1))
            def _():
                j = mirrored(d, jm)

                @pl.when(zm > 0)
                def _():
                    rs_wait(d, j, q)
                    acc[j, q] = acc[j, q] + rbuf[j, q]
                rs_copy(d, j, q).start()
            return carry
        lax.fori_loop(0, 2, one, 0)

    def main_step(i, carry):
        s, q = i // n_q, i % n_q

        @pl.when(s > 0)
        def _():
            gather_step(s, q)
        compute_step(s, q)
        reduce_step(s, q)
        return carry
    lax.fori_loop(0, n * n_q, main_step, 0)

    win_t = win32.T
    window_sum = jnp.zeros((wsize, core.shape[1]), jnp.float32)
    core_sum = jnp.zeros(core.shape, jnp.float32)
    small_ref[pl.ds(wsize + core.shape[0], 8), :] = jnp.zeros((8, core.shape[1]), jnp.float32)
    for m in range(months):
        drow = jnp.broadcast_to(scales[m:m + 1, :], core.shape)
        dcol = drow.T
        inner = dcol * core[...] * drow
        window_sum += lax.dot_general(fmat[m], inner, (((1,), (1,)), ((), ())),
                                      precision=HIGHEST, preferred_element_type=jnp.float32)
        gram = jnp.dot(win_t, fmat[m], precision=HIGHEST, preferred_element_type=jnp.float32)
        core_sum += dcol * gram * drow
        weighted = gram * core[...]
        by_row = jnp.sum(weighted.T * dcol, axis=0, keepdims=True)
        by_col = jnp.sum(weighted * dcol, axis=0, keepdims=True)
        small_ref[pl.ds(wsize + core.shape[0] + m, 1), :] = -coef * (by_row + by_col)
    small_ref[pl.ds(0, wsize), :] = -coef * window_sum
    small_ref[pl.ds(wsize, core.shape[0]), :] = -coef * core_sum

    def tail_step(i, carry):
        reduce_step(i // n_q, i % n_q)
        return carry
    lax.fori_loop(n * n_q, (2 * n - 1) * n_q, tail_step, 0)

    for q in range(n_q):
        @pl.when(z > 0)
        def _():
            rs_wait(0, z, q)
            acc[z, q] = acc[z, q] + rbuf[z, q]

        @pl.when(z < n - 1)
        def _():
            rs_wait(1, n, q)
            acc[z, q] = acc[z, q] + rbuf[n, q]
        grad_ref[pl.ds(q * r, r), :] = -coef * acc[z, q].T

    def drain(i, carry):
        j, q = i // n_q, i % n_q
        remote_trade(j, q).wait_send()

        @pl.when((j <= z) & (z < n - 1))
        def _():
            ag_copy(0, j, q).wait_send()

        @pl.when((j >= z) & (z > 0))
        def _():
            ag_copy(1, j, q).wait_send()

        @pl.when(j != z)
        def _():
            rs_copy(jnp.where(j > z, 0, 1), j, q).wait_send()
        return carry
    lax.fori_loop(0, n * n_q, drain, 0)

    @pl.when(t == 0)
    def _():
        for p in range(pieces):
            @pl.when(z < n - 1)
            def _():
                win_up(p).wait_send()
            for k in range(1, tiles):
                win_side(p, k).wait_send()


def fused(n, tiles, trade, factor, scales, core):
    months, rows, size = trade.shape[0], trade.shape[2], factor.shape[1]
    shard = factor.shape[0]
    r = 256
    n_q = shard // r
    wsize = 2 * rows
    pieces = wsize // r
    coef = 1.0 / math.sqrt(months * n * wsize)
    vmem = pl.BlockSpec(memory_space=pltpu.VMEM)
    anyspace = pl.BlockSpec(memory_space=pl.ANY)
    dma = pltpu.SemaphoreType.DMA
    return pl.pallas_call(
        functools.partial(kernel, n, tiles, coef),
        out_shape=(jax.ShapeDtypeStruct((shard, size), jnp.float32),
                   jax.ShapeDtypeStruct((wsize + size + 8, size), jnp.float32)),
        in_specs=[anyspace, anyspace, vmem, vmem],
        out_specs=(vmem, vmem),
        scratch_shapes=[
            pltpu.VMEM((n, n_q, months, 2, rows, r), jnp.bfloat16),
            pltpu.VMEM((n, n_q, r, size), jnp.bfloat16),
            pltpu.VMEM((wsize, size), jnp.bfloat16),
            pltpu.VMEM((n, n_q, size, r), jnp.float32),
            pltpu.VMEM((n + 1, n_q, size, r), jnp.float32),
            pltpu.VMEM((months, wsize, size), jnp.float32),
            pltpu.VMEM((months, wsize, size), jnp.bfloat16),
            pltpu.VMEM((months, size, wsize), jnp.bfloat16),
            dma((n, n_q)), dma((n, n_q)), dma((n, n_q)), dma((n_q,)),
            dma((2, n, n_q)), dma((n, n_q)), dma((n, n_q)), dma((n + 1, n_q)),
            dma((pieces, tiles)), dma((pieces,)),
        ],
        compiler_params=pltpu.CompilerParams(
            collective_id=0, has_side_effects=True, vmem_limit_bytes=56 * 2**20),
    )(trade, factor, scales, core)


def small_sums(n, small, wsize, size, months):
    z = lax.axis_index("cuts")
    diag = jnp.zeros((months * n, size), jnp.float32)
    diag = lax.dynamic_update_slice_in_dim(
        diag, small[wsize + size:wsize + size + months], z * months, 0)
    total = lax.psum(jnp.concatenate([small[:wsize + size], diag], 0), ("tile", "cuts"))
    window = lax.dynamic_slice_in_dim(total, z * (wsize // n), wsize // n, 0)
    diag = lax.dynamic_slice_in_dim(total, wsize + size + z * months, months, 0)
    return window, total[wsize:wsize + size], diag


def swapped(value, axis, distance):
    mask = 2**distance
    pairs = [(source, source ^ mask) for source in range(lax.axis_size(axis))]
    return lax.ppermute(value, axis, pairs)


def plain(trade, factor, scales, core):
    n = lax.axis_size("cuts")
    band_index = lax.axis_index("tile") % 2
    months, rows, size = trade.shape[0], trade.shape[2], factor.shape[1]
    wsize = 2 * rows
    own = lax.all_gather(factor, "cuts", axis=0, tiled=True)
    block = own.shape[0]
    partner = swapped(own, "tile", 0)
    columns = jnp.concatenate([jnp.where(band_index == 0, own, partner),
                               jnp.where(band_index == 0, partner, own)], 0)
    first = jnp.where(lax.axis_index("tile") == 0, own[:wsize], jnp.zeros_like(own[:wsize]))
    window = lax.psum(first, "tile")
    window32 = lax.dynamic_slice_in_dim(window, band_index * rows, rows, 0).astype(jnp.float32)
    coef = 1.0 / math.sqrt(months * n * wsize)
    acc_columns = jnp.zeros((2 * block, size), jnp.float32)
    acc_window = jnp.zeros((rows, size), jnp.float32)
    acc_core = jnp.zeros((size, size), jnp.float32)
    diags = []
    for month in range(months):
        diag_k = scales[month]
        inner = diag_k[:, None] * core * diag_k[None, :]
        mapped = jnp.dot(window32, inner, precision=HIGHEST).astype(jnp.bfloat16)
        model = lax.dot_general(mapped, columns, (((1,), (1,)), ((), ())),
                                preferred_element_type=jnp.float32)
        residual = (trade[month, 0].astype(jnp.float32) - model).astype(jnp.bfloat16)
        acc_columns = acc_columns + lax.dot_general(
            residual, mapped, (((0,), (0,)), ((), ())), preferred_element_type=jnp.float32)
        projected = jnp.dot(residual, columns, preferred_element_type=jnp.float32)
        acc_window = acc_window + jnp.dot(projected, inner.T, precision=HIGHEST)
        gram = jnp.dot(window32.T, projected, precision=HIGHEST)
        acc_core = acc_core + diag_k[:, None] * gram * diag_k[None, :]
        weighted = gram * core
        diags.append(jnp.dot(weighted, diag_k, precision=HIGHEST)
                     + jnp.dot(weighted.T, diag_k, precision=HIGHEST))
    halves = acc_columns.reshape(2, block, size)
    mine = jnp.where(band_index == 0, halves[0], halves[1])
    other = jnp.where(band_index == 0, halves[1], halves[0])
    grad = lax.psum_scatter(mine + swapped(other, "tile", 0), "cuts",
                            scatter_dimension=0, tiled=True)
    padded = lax.dynamic_update_slice_in_dim(
        jnp.zeros((wsize, size), jnp.float32), acc_window, band_index * rows, 0)
    small = jnp.concatenate([padded, acc_core, jnp.stack(diags, 0)], 0)
    window, core_total, diag = small_sums(n, -coef * small, wsize, size, months)
    return -coef * grad, window, core_total, diag


def body(trade, factor, scales, core):
    n, tiles = lax.axis_size("cuts"), lax.axis_size("tile")
    months, wsize, size = trade.shape[0], 2 * trade.shape[2], factor.shape[1]
    if factor.shape[0] % 256 or factor.shape[0] < wsize or n < 2:
        return plain(trade, factor, scales, core)
    grad, small = fused(n, tiles, trade, factor, scales, core)
    window, core_total, diag = small_sums(n, small, wsize, size, months)
    return grad, window, core_total, diag


def solution(mesh):
    return jax.shard_map(
        body,
        mesh=mesh,
        in_specs=(
            P(("groups", "cuts"), "tile", None, None),
            P(("groups", "tile", "cuts"), None),
            P(("groups", "cuts"), None),
            P("groups", None),
        ),
        out_specs=(
            P(("groups", "tile", "cuts"), None),
            P(("groups", "cuts"), None),
            P("groups", None),
            P(("groups", "cuts"), None),
        ),
        check_vma=False,
    )
```

```python
import functools
import math

import jax
import jax.numpy as jnp
from jax import lax
from jax.experimental import pallas as pl
from jax.experimental.pallas import tpu as pltpu
from jax.sharding import PartitionSpec as P

HIGHEST = lax.Precision.HIGHEST
MESH = pl.DeviceIdType.MESH


def kernel(n, tiles, coef, trade, factor, scales, core, grad_ref, wout_ref, core_ref, diag_ref,
           tv, fac, win, acc, rbuf, fmat, bmat, bmat_t,
           part, p1buf, s2, p2buf, cfin, wfin, dbuf,
           tl_sem, ts_sem, tr_sem, own_sem, ag_send, ag_recv, rs_send, rs_recv, win_send, win_recv,
           p1_send, p1_recv, p2_send, p2_recv, p3_send, p3_recv, p4_send, p4_recv, p5_send, p5_recv,
           d_send, d_recv):
    z = lax.axis_index("cuts")
    t = lax.axis_index("tile")
    c = lax.rem(t, 2)
    partner = t + 1 - 2 * c
    months = trade.shape[0]
    rows = trade.shape[2]
    n_q, r = fac.shape[1], fac.shape[2]
    shard = n_q * r
    block = n * shard
    wsize = win.shape[0]
    pieces = win_recv.shape[0]
    wrow = wsize // pieces

    barrier = pltpu.get_barrier_semaphore()

    for k in range(1, n):
        pl.semaphore_signal(
            barrier, inc=1, device_id={"cuts": lax.rem(z + k, n)}, device_id_type=MESH)
    for k in range(1, tiles):
        pl.semaphore_signal(
            barrier, inc=1, device_id={"tile": lax.rem(t + k, tiles)}, device_id_type=MESH)

    def own_copy(q):
        return pltpu.make_async_copy(factor.at[pl.ds(q * r, r)], fac.at[z, q], own_sem.at[q])

    def local_trade(j, q):
        off = pl.multiple_of(c * block + j * shard + q * r, 128)
        return pltpu.make_async_copy(
            trade.at[:, 0, :, pl.ds(off, r)], tv.at[j, q, :, c], tl_sem.at[j, q])

    def remote_trade(j, q):
        off = pl.multiple_of((1 - c) * block + j * shard + q * r, 128)
        return pltpu.make_async_remote_copy(
            src_ref=trade.at[:, 0, :, pl.ds(off, r)], dst_ref=tv.at[j, q, :, c],
            send_sem=ts_sem.at[j, q], recv_sem=tr_sem.at[j, q],
            device_id={"tile": partner}, device_id_type=MESH)

    def recv_trade(j, q):
        off = pl.multiple_of(c * block + j * shard + q * r, 128)
        return pltpu.make_async_remote_copy(
            src_ref=trade.at[:, 0, :, pl.ds(off, r)], dst_ref=tv.at[j, q, :, 1 - c],
            send_sem=ts_sem.at[j, q], recv_sem=tr_sem.at[j, q],
            device_id={"tile": partner}, device_id_type=MESH)

    for q in range(n_q):
        own_copy(q).start()

    pl.semaphore_wait(barrier, tiles + n - 2)
    for q in range(n_q):
        own_copy(q).wait()

    def win_up(p):
        return pltpu.make_async_remote_copy(
            src_ref=win.at[pl.ds(p * wrow, wrow)], dst_ref=win.at[pl.ds(p * wrow, wrow)],
            send_sem=win_send.at[p, 0], recv_sem=win_recv.at[p],
            device_id={"cuts": z + 1}, device_id_type=MESH)

    def win_side(p, k):
        return pltpu.make_async_remote_copy(
            src_ref=win.at[pl.ds(p * wrow, wrow)], dst_ref=win.at[pl.ds(p * wrow, wrow)],
            send_sem=win_send.at[p, k], recv_sem=win_recv.at[p],
            device_id={"tile": k}, device_id_type=MESH)

    def win_recv_wait(p):
        win_up(p).wait_recv()

    @pl.when((t == 0) & (z == 0))
    def _():
        for p in range(pieces):
            win[pl.ds(p * wrow, wrow), :] = fac[0, p]

    @pl.when((t == 0) & (z == 0))
    def _():
        for p in range(pieces):
            if n > 1:
                win_up(p).start()
            for k in range(1, tiles):
                win_side(p, k).start()

    def mirrored(d, x):
        return jnp.where(d == 0, x, n - 1 - x)

    def ag_copy(d, j, q):
        return pltpu.make_async_remote_copy(
            src_ref=fac.at[j, q], dst_ref=fac.at[j, q],
            send_sem=ag_send.at[d, j, q], recv_sem=ag_recv.at[j, q],
            device_id={"cuts": z + 1 - 2 * d}, device_id_type=MESH)

    def gather_step(s, q):
        def one(d, carry):
            zm = mirrored(d, z)
            jm = zm - s

            @pl.when(jm >= 0)
            def _():
                j = mirrored(d, jm)

                @pl.when(s > 0)
                def _():
                    ag_copy(d, j, q).wait_recv()

                @pl.when(zm < n - 1)
                def _():
                    ag_copy(d, j, q).start()
            return carry
        lax.fori_loop(0, 2, one, 0)

    def gather_first(q, carry):
        gather_step(0, q)
        return carry
    lax.fori_loop(0, n_q, gather_first, 0)

    def trade_start(i, carry):
        s, q = i // n_q, i % n_q
        for d in (0, 1):
            zm = mirrored(d, z)

            @pl.when((zm - s >= 0) & ((s > 0) | (d == 0)))
            def _():
                j = mirrored(d, zm - s)
                local_trade(j, q).start()
                remote_trade(j, q).start()
        return carry
    lax.fori_loop(0, n * n_q, trade_start, 0)

    @pl.when((t != 0) | (z != 0))
    def _():
        for p in range(pieces):
            win_recv_wait(p)

            @pl.when(t == 0)
            def _():
                @pl.when(z < n - 1)
                def _():
                    win_up(p).start()
                for k in range(1, tiles):
                    win_side(p, k).start()

    def inner_of(m):
        drow = jnp.broadcast_to(scales[m:m + 1, :], core.shape)
        return drow.T * core[...] * drow

    win32 = win[...].astype(jnp.float32)
    for m in range(months):
        mapped = jnp.dot(win32, inner_of(m), precision=HIGHEST,
                         preferred_element_type=jnp.float32)
        bmat[m] = mapped.astype(jnp.bfloat16)
        bmat_t[m] = mapped.T.astype(jnp.bfloat16)
        fmat[m] = jnp.zeros_like(fmat[m])

    def compute(j, q):
        local_trade(j, q).wait()
        recv_trade(j, q).wait_recv()
        a = fac[j, q]
        total = None
        for m in range(months):
            x = jnp.concatenate([tv[j, q, m, 0], tv[j, q, m, 1]], 0)
            model = lax.dot_general(bmat[m], a, (((1,), (1,)), ((), ())),
                                    preferred_element_type=jnp.float32)
            e = (x.astype(jnp.float32) - model).astype(jnp.bfloat16)
            term = jnp.dot(bmat_t[m], e, preferred_element_type=jnp.float32)
            total = term if total is None else total + term
            fmat[m] += jnp.dot(e, a, preferred_element_type=jnp.float32)
        acc[j, q] = total

    def compute_step(s, q):
        def one(d, carry):
            jm = mirrored(d, z) - s

            @pl.when((jm >= 0) & ((s > 0) | (d == 0)))
            def _():
                compute(mirrored(d, jm), q)
            return carry
        lax.fori_loop(0, 2, one, 0)

    def rs_copy(d, j, q):
        to = z + 1 - 2 * d
        slot = jnp.where((j == to) & (d == 1), n, j)
        return pltpu.make_async_remote_copy(
            src_ref=acc.at[j, q], dst_ref=rbuf.at[slot, q],
            send_sem=rs_send.at[j, q], recv_sem=rs_recv.at[slot, q],
            device_id={"cuts": to}, device_id_type=MESH)

    def rs_wait(d, slot, q):
        pltpu.make_async_remote_copy(
            src_ref=acc.at[0, q], dst_ref=rbuf.at[slot, q],
            send_sem=rs_send.at[0, q], recv_sem=rs_recv.at[slot, q],
            device_id={"cuts": z + 1 - 2 * d}, device_id_type=MESH).wait_recv()

    def reduce_step(s, q):
        def one(d, carry):
            zm = mirrored(d, z)
            jm = s - zm

            @pl.when((jm > zm) & (jm <= n - 1))
            def _():
                j = mirrored(d, jm)

                @pl.when(zm > 0)
                def _():
                    rs_wait(d, j, q)
                    acc[j, q] = acc[j, q] + rbuf[j, q]
                rs_copy(d, j, q).start()
            return carry
        lax.fori_loop(0, 2, one, 0)

    def main_step(i, carry):
        s, q = i // n_q, i % n_q

        @pl.when(s > 0)
        def _():
            gather_step(s, q)
        compute_step(s, q)
        reduce_step(s, q)
        return carry
    lax.fori_loop(0, n * n_q, main_step, 0)

    win_t = win32.T
    window_sum = jnp.zeros((wsize, core.shape[1]), jnp.float32)
    core_sum = jnp.zeros(core.shape, jnp.float32)
    diags = []
    for m in range(months):
        drow = jnp.broadcast_to(scales[m:m + 1, :], core.shape)
        dcol = drow.T
        inner = dcol * core[...] * drow
        window_sum += lax.dot_general(fmat[m], inner, (((1,), (1,)), ((), ())),
                                      precision=HIGHEST, preferred_element_type=jnp.float32)
        gram = jnp.dot(win_t, fmat[m], precision=HIGHEST, preferred_element_type=jnp.float32)
        core_sum += dcol * gram * drow
        weighted = gram * core[...]
        by_row = jnp.sum(weighted.T * dcol, axis=0, keepdims=True)
        by_col = jnp.sum(weighted * dcol, axis=0, keepdims=True)
        diags.append(-coef * (by_row + by_col))
    wr, cr = wfin.shape[1], cfin.shape[2]
    for k in range(tiles):
        for i in range(n):
            w0, c0 = (i * tiles + k) * wr, (i * tiles + k) * cr
            part[k, i, pl.ds(0, wr), :] = -coef * window_sum[w0:w0 + wr]
            part[k, i, pl.ds(wr, cr), :] = -coef * core_sum[c0:c0 + cr]
    dbuf[t] = jnp.concatenate(
        diags + [jnp.zeros((8 - months, core.shape[1]), jnp.float32)], 0)

    def peer_t(k):
        return lax.rem(t + k, tiles)

    def peer_z(k):
        return lax.rem(z + k, n)

    def to_tile(src, dst, send, recv, k, who):
        return pltpu.make_async_remote_copy(
            src_ref=src, dst_ref=dst, send_sem=send.at[k], recv_sem=recv.at[who],
            device_id={"tile": peer_t(k)}, device_id_type=MESH)

    def to_cut(src, dst, send, recv, k, who):
        return pltpu.make_async_remote_copy(
            src_ref=src, dst_ref=dst, send_sem=send.at[k], recv_sem=recv.at[who],
            device_id={"cuts": peer_z(k)}, device_id_type=MESH)

    def p1(k, who):
        return to_tile(part.at[peer_t(k)], p1buf.at[who], p1_send, p1_recv, k, who)

    def pd(k, who):
        return to_tile(dbuf.at[who], dbuf.at[who], d_send, d_recv, k, who)

    def p2(k, who):
        return to_cut(s2.at[peer_z(k)], p2buf.at[who], p2_send, p2_recv, k, who)

    def p3(k, who):
        return to_cut(cfin.at[who, t], cfin.at[who, t], p3_send, p3_recv, k, who)

    def p4(k, who):
        return to_tile(cfin.at[:, who], cfin.at[:, who], p4_send, p4_recv, k, who)

    def p5(k, who):
        return to_tile(wfin.at[who], wfin.at[who], p5_send, p5_recv, k, who)

    for k in range(1, tiles):
        p1(k, t).start()
        pd(k, t).start()

    def small_second():
        for k in range(1, tiles):
            p1(k, peer_t(k)).wait_recv()
        total = part[t]
        for k in range(1, tiles):
            total = total + p1buf[peer_t(k)]
        s2[...] = total
        for k in range(1, n):
            p2(k, z).start()

    def small_third():
        for k in range(1, n):
            p2(k, peer_z(k)).wait_recv()
        total = s2[z]
        for k in range(1, n):
            total = total + p2buf[peer_z(k)]
        wfin[t] = total[:wr]
        cfin[z, t] = total[wr:]
        for k in range(1, n):
            p3(k, z).start()
        for k in range(1, tiles):
            p5(k, t).start()

    def small_fourth():
        for k in range(1, n):
            p3(k, peer_z(k)).wait_recv()
        for k in range(1, tiles):
            p4(k, t).start()

    def small_last():
        for k in range(1, tiles):
            p4(k, peer_t(k)).wait_recv()
            p5(k, peer_t(k)).wait_recv()
            pd(k, peer_t(k)).wait_recv()
        for k in range(tiles):
            wout_ref[pl.ds(k * wr, wr), :] = wfin[k]
            for i in range(n):
                core_ref[pl.ds((i * tiles + k) * cr, cr), :] = cfin[i, k]
        total = dbuf[0]
        for k in range(1, tiles):
            total = total + dbuf[k]
        diag_ref[...] = total[:months]
        for k in range(1, tiles):
            p1(k, t).wait_send()
            pd(k, t).wait_send()
            p4(k, t).wait_send()
            p5(k, t).wait_send()
        for k in range(1, n):
            p2(k, z).wait_send()
            p3(k, z).wait_send()

    def tail_step(i, carry):
        reduce_step(i // n_q, i % n_q)
        return carry

    stages = [small_second, small_third, small_fourth]
    for s in range(n, 2 * n - 1):
        lax.fori_loop(s * n_q, (s + 1) * n_q, tail_step, 0)
        if stages:
            stages.pop(0)()
    for stage in stages:
        stage()

    for q in range(n_q):
        @pl.when(z > 0)
        def _():
            rs_wait(0, z, q)
            acc[z, q] = acc[z, q] + rbuf[z, q]

        @pl.when(z < n - 1)
        def _():
            rs_wait(1, n, q)
            acc[z, q] = acc[z, q] + rbuf[n, q]
        grad_ref[pl.ds(q * r, r), :] = -coef * acc[z, q].T

    small_last()

    def drain(i, carry):
        j, q = i // n_q, i % n_q
        remote_trade(j, q).wait_send()

        @pl.when((j <= z) & (z < n - 1))
        def _():
            ag_copy(0, j, q).wait_send()

        @pl.when((j >= z) & (z > 0))
        def _():
            ag_copy(1, j, q).wait_send()

        @pl.when(j != z)
        def _():
            rs_copy(jnp.where(j > z, 0, 1), j, q).wait_send()
        return carry
    lax.fori_loop(0, n * n_q, drain, 0)

    @pl.when(t == 0)
    def _():
        for p in range(pieces):
            @pl.when(z < n - 1)
            def _():
                win_up(p).wait_send()
            for k in range(1, tiles):
                win_side(p, k).wait_send()


def fused(n, tiles, trade, factor, scales, core):
    months, rows, size = trade.shape[0], trade.shape[2], factor.shape[1]
    shard = factor.shape[0]
    r = 256
    n_q = shard // r
    wsize = 2 * rows
    pieces = wsize // r
    wr, cr = wsize // (n * tiles), size // (n * tiles)
    coef = 1.0 / math.sqrt(months * n * wsize)
    vmem = pl.BlockSpec(memory_space=pltpu.VMEM)
    anyspace = pl.BlockSpec(memory_space=pl.ANY)
    dma = pltpu.SemaphoreType.DMA
    return pl.pallas_call(
        functools.partial(kernel, n, tiles, coef),
        out_shape=(jax.ShapeDtypeStruct((shard, size), jnp.float32),
                   jax.ShapeDtypeStruct((wsize // n, size), jnp.float32),
                   jax.ShapeDtypeStruct((size, size), jnp.float32),
                   jax.ShapeDtypeStruct((months, size), jnp.float32)),
        in_specs=[anyspace, anyspace, vmem, vmem],
        out_specs=(vmem, vmem, vmem, vmem),
        scratch_shapes=[
            pltpu.VMEM((n, n_q, months, 2, rows, r), jnp.bfloat16),
            pltpu.VMEM((n, n_q, r, size), jnp.bfloat16),
            pltpu.VMEM((wsize, size), jnp.bfloat16),
            pltpu.VMEM((n, n_q, size, r), jnp.float32),
            pltpu.VMEM((n + 1, n_q, size, r), jnp.float32),
            pltpu.VMEM((months, wsize, size), jnp.float32),
            pltpu.VMEM((months, wsize, size), jnp.bfloat16),
            pltpu.VMEM((months, size, wsize), jnp.bfloat16),
            pltpu.VMEM((tiles, n, wr + cr, size), jnp.float32),
            pltpu.VMEM((tiles, n, wr + cr, size), jnp.float32),
            pltpu.VMEM((n, wr + cr, size), jnp.float32),
            pltpu.VMEM((n, wr + cr, size), jnp.float32),
            pltpu.VMEM((n, tiles, cr, size), jnp.float32),
            pltpu.VMEM((tiles, wr, size), jnp.float32),
            pltpu.VMEM((tiles, 8, size), jnp.float32),
            dma((n, n_q)), dma((n, n_q)), dma((n, n_q)), dma((n_q,)),
            dma((2, n, n_q)), dma((n, n_q)), dma((n, n_q)), dma((n + 1, n_q)),
            dma((pieces, tiles)), dma((pieces,)),
            dma((tiles,)), dma((tiles,)), dma((n,)), dma((n,)), dma((n,)), dma((n,)),
            dma((tiles,)), dma((tiles,)), dma((tiles,)), dma((tiles,)), dma((tiles,)), dma((tiles,)),
        ],
        compiler_params=pltpu.CompilerParams(
            collective_id=0, has_side_effects=True, vmem_limit_bytes=56 * 2**20),
    )(trade, factor, scales, core)


def small_sums(n, small, wsize, size, months):
    z = lax.axis_index("cuts")
    diag = jnp.zeros((months * n, size), jnp.float32)
    diag = lax.dynamic_update_slice_in_dim(
        diag, small[wsize + size:wsize + size + months], z * months, 0)
    total = lax.psum(jnp.concatenate([small[:wsize + size], diag], 0), ("tile", "cuts"))
    window = lax.dynamic_slice_in_dim(total, z * (wsize // n), wsize // n, 0)
    diag = lax.dynamic_slice_in_dim(total, wsize + size + z * months, months, 0)
    return window, total[wsize:wsize + size], diag


def swapped(value, axis, distance):
    mask = 2**distance
    pairs = [(source, source ^ mask) for source in range(lax.axis_size(axis))]
    return lax.ppermute(value, axis, pairs)


def plain(trade, factor, scales, core):
    n = lax.axis_size("cuts")
    band_index = lax.axis_index("tile") % 2
    months, rows, size = trade.shape[0], trade.shape[2], factor.shape[1]
    wsize = 2 * rows
    own = lax.all_gather(factor, "cuts", axis=0, tiled=True)
    block = own.shape[0]
    partner = swapped(own, "tile", 0)
    columns = jnp.concatenate([jnp.where(band_index == 0, own, partner),
                               jnp.where(band_index == 0, partner, own)], 0)
    first = jnp.where(lax.axis_index("tile") == 0, own[:wsize], jnp.zeros_like(own[:wsize]))
    window = lax.psum(first, "tile")
    window32 = lax.dynamic_slice_in_dim(window, band_index * rows, rows, 0).astype(jnp.float32)
    coef = 1.0 / math.sqrt(months * n * wsize)
    acc_columns = jnp.zeros((2 * block, size), jnp.float32)
    acc_window = jnp.zeros((rows, size), jnp.float32)
    acc_core = jnp.zeros((size, size), jnp.float32)
    diags = []
    for month in range(months):
        diag_k = scales[month]
        inner = diag_k[:, None] * core * diag_k[None, :]
        mapped = jnp.dot(window32, inner, precision=HIGHEST).astype(jnp.bfloat16)
        model = lax.dot_general(mapped, columns, (((1,), (1,)), ((), ())),
                                preferred_element_type=jnp.float32)
        residual = (trade[month, 0].astype(jnp.float32) - model).astype(jnp.bfloat16)
        acc_columns = acc_columns + lax.dot_general(
            residual, mapped, (((0,), (0,)), ((), ())), preferred_element_type=jnp.float32)
        projected = jnp.dot(residual, columns, preferred_element_type=jnp.float32)
        acc_window = acc_window + jnp.dot(projected, inner.T, precision=HIGHEST)
        gram = jnp.dot(window32.T, projected, precision=HIGHEST)
        acc_core = acc_core + diag_k[:, None] * gram * diag_k[None, :]
        weighted = gram * core
        diags.append(jnp.dot(weighted, diag_k, precision=HIGHEST)
                     + jnp.dot(weighted.T, diag_k, precision=HIGHEST))
    halves = acc_columns.reshape(2, block, size)
    mine = jnp.where(band_index == 0, halves[0], halves[1])
    other = jnp.where(band_index == 0, halves[1], halves[0])
    grad = lax.psum_scatter(mine + swapped(other, "tile", 0), "cuts",
                            scatter_dimension=0, tiled=True)
    padded = lax.dynamic_update_slice_in_dim(
        jnp.zeros((wsize, size), jnp.float32), acc_window, band_index * rows, 0)
    small = jnp.concatenate([padded, acc_core, jnp.stack(diags, 0)], 0)
    window, core_total, diag = small_sums(n, -coef * small, wsize, size, months)
    return -coef * grad, window, core_total, diag


def body(trade, factor, scales, core):
    n, tiles = lax.axis_size("cuts"), lax.axis_size("tile")
    months, wsize, size = trade.shape[0], 2 * trade.shape[2], factor.shape[1]
    if factor.shape[0] % 256 or factor.shape[0] < wsize or n < 2 or months > 8:
        return plain(trade, factor, scales, core)
    if wsize % (8 * n * tiles) or size % (8 * n * tiles):
        return plain(trade, factor, scales, core)
    return fused(n, tiles, trade, factor, scales, core)


def solution(mesh):
    return jax.shard_map(
        body,
        mesh=mesh,
        in_specs=(
            P(("groups", "cuts"), "tile", None, None),
            P(("groups", "tile", "cuts"), None),
            P(("groups", "cuts"), None),
            P("groups", None),
        ),
        out_specs=(
            P(("groups", "tile", "cuts"), None),
            P(("groups", "cuts"), None),
            P("groups", None),
            P(("groups", "cuts"), None),
        ),
        check_vma=False,
    )
```

```python
import functools
import math

import jax
import jax.numpy as jnp
from jax import lax
from jax.experimental import pallas as pl
from jax.experimental.pallas import tpu as pltpu
from jax.sharding import PartitionSpec as P

HIGHEST = lax.Precision.HIGHEST
MESH = pl.DeviceIdType.MESH


SPAN = 250.0


def encode(ref, x):
    size = x.shape[0]
    top = jnp.maximum(jnp.max(jnp.abs(x), axis=0, keepdims=True), 1e-30)
    scale = (top * 1.008).astype(jnp.bfloat16).astype(jnp.float32)
    u = x * (1.0 / scale)
    a = jnp.exp2(jnp.abs(u) * SPAN - 0.5 * SPAN)
    ref[pl.ds(0, size), :] = jnp.where(u < 0.0, -a, a).astype(jnp.bfloat16)
    ref[pl.ds(size, 16), :] = jnp.broadcast_to(scale, (16, x.shape[1])).astype(jnp.bfloat16)


def decode(ref):
    size = ref.shape[0] - 16
    y = ref[pl.ds(0, size), :].astype(jnp.float32)
    scale = ref[pl.ds(size, 16), :].astype(jnp.float32)[:1]
    u = jnp.log(jnp.abs(y)) * (1.0 / (SPAN * math.log(2.0))) + 0.5
    return jnp.where(y < 0.0, -u, u) * scale


def kernel(n, tiles, coef, trade, factor, scales, core, grad_ref, wout_ref, core_ref, diag_ref,
           tv, fac, win, acc, sbuf, rbuf, fmat, bmat, bmat_t,
           part, p1buf, s2, p2buf, cfin, wfin, dbuf,
           tl_sem, ts_sem, tr_sem, own_sem, ag_send, ag_recv, rs_send, rs_recv, win_send, win_recv,
           p1_send, p1_recv, p2_send, p2_recv, p3_send, p3_recv, p4_send, p4_recv, p5_send, p5_recv,
           d_send, d_recv):
    z = lax.axis_index("cuts")
    t = lax.axis_index("tile")
    c = lax.rem(t, 2)
    partner = t + 1 - 2 * c
    months = trade.shape[0]
    rows = trade.shape[2]
    n_q, r = fac.shape[1], fac.shape[2]
    shard = n_q * r
    block = n * shard
    wsize = win.shape[0]
    pieces = win_recv.shape[0]
    wrow = wsize // pieces

    barrier = pltpu.get_barrier_semaphore()

    for k in range(1, n):
        pl.semaphore_signal(
            barrier, inc=1, device_id={"cuts": lax.rem(z + k, n)}, device_id_type=MESH)
    for k in range(1, tiles):
        pl.semaphore_signal(
            barrier, inc=1, device_id={"tile": lax.rem(t + k, tiles)}, device_id_type=MESH)

    def own_copy(q):
        return pltpu.make_async_copy(factor.at[pl.ds(q * r, r)], fac.at[z, q], own_sem.at[q])

    def local_trade(j, q):
        off = pl.multiple_of(c * block + j * shard + q * r, 128)
        return pltpu.make_async_copy(
            trade.at[:, 0, :, pl.ds(off, r)], tv.at[j, q, :, c], tl_sem.at[j, q])

    def remote_trade(j, q):
        off = pl.multiple_of((1 - c) * block + j * shard + q * r, 128)
        return pltpu.make_async_remote_copy(
            src_ref=trade.at[:, 0, :, pl.ds(off, r)], dst_ref=tv.at[j, q, :, c],
            send_sem=ts_sem.at[j, q], recv_sem=tr_sem.at[j, q],
            device_id={"tile": partner}, device_id_type=MESH)

    def recv_trade(j, q):
        off = pl.multiple_of(c * block + j * shard + q * r, 128)
        return pltpu.make_async_remote_copy(
            src_ref=trade.at[:, 0, :, pl.ds(off, r)], dst_ref=tv.at[j, q, :, 1 - c],
            send_sem=ts_sem.at[j, q], recv_sem=tr_sem.at[j, q],
            device_id={"tile": partner}, device_id_type=MESH)

    for q in range(n_q):
        own_copy(q).start()

    pl.semaphore_wait(barrier, tiles + n - 2)
    for q in range(n_q):
        own_copy(q).wait()

    def win_up(p):
        return pltpu.make_async_remote_copy(
            src_ref=win.at[pl.ds(p * wrow, wrow)], dst_ref=win.at[pl.ds(p * wrow, wrow)],
            send_sem=win_send.at[p, 0], recv_sem=win_recv.at[p],
            device_id={"cuts": z + 1}, device_id_type=MESH)

    def win_side(p, k):
        return pltpu.make_async_remote_copy(
            src_ref=win.at[pl.ds(p * wrow, wrow)], dst_ref=win.at[pl.ds(p * wrow, wrow)],
            send_sem=win_send.at[p, k], recv_sem=win_recv.at[p],
            device_id={"tile": k}, device_id_type=MESH)

    def win_recv_wait(p):
        win_up(p).wait_recv()

    @pl.when((t == 0) & (z == 0))
    def _():
        for p in range(pieces):
            win[pl.ds(p * wrow, wrow), :] = fac[0, p]

    @pl.when((t == 0) & (z == 0))
    def _():
        for p in range(pieces):
            if n > 1:
                win_up(p).start()
            for k in range(1, tiles):
                win_side(p, k).start()

    def mirrored(d, x):
        return jnp.where(d == 0, x, n - 1 - x)

    def ag_copy(d, j, q):
        return pltpu.make_async_remote_copy(
            src_ref=fac.at[j, q], dst_ref=fac.at[j, q],
            send_sem=ag_send.at[d, j, q], recv_sem=ag_recv.at[j, q],
            device_id={"cuts": z + 1 - 2 * d}, device_id_type=MESH)

    def gather_step(s, q):
        def one(d, carry):
            zm = mirrored(d, z)
            jm = zm - s

            @pl.when(jm >= 0)
            def _():
                j = mirrored(d, jm)

                @pl.when(s > 0)
                def _():
                    ag_copy(d, j, q).wait_recv()

                @pl.when(zm < n - 1)
                def _():
                    ag_copy(d, j, q).start()
            return carry
        lax.fori_loop(0, 2, one, 0)

    def gather_first(q, carry):
        gather_step(0, q)
        return carry
    lax.fori_loop(0, n_q, gather_first, 0)

    def trade_start(i, carry):
        s, q = i // n_q, i % n_q
        for d in (0, 1):
            zm = mirrored(d, z)

            @pl.when((zm - s >= 0) & ((s > 0) | (d == 0)))
            def _():
                j = mirrored(d, zm - s)
                local_trade(j, q).start()
                remote_trade(j, q).start()
        return carry
    lax.fori_loop(0, n * n_q, trade_start, 0)

    @pl.when((t != 0) | (z != 0))
    def _():
        for p in range(pieces):
            win_recv_wait(p)

            @pl.when(t == 0)
            def _():
                @pl.when(z < n - 1)
                def _():
                    win_up(p).start()
                for k in range(1, tiles):
                    win_side(p, k).start()

    def inner_of(m):
        drow = jnp.broadcast_to(scales[m:m + 1, :], core.shape)
        return drow.T * core[...] * drow

    win32 = win[...].astype(jnp.float32)
    for m in range(months):
        mapped = jnp.dot(win32, inner_of(m), precision=HIGHEST,
                         preferred_element_type=jnp.float32)
        bmat[m] = mapped.astype(jnp.bfloat16)
        bmat_t[m] = mapped.T.astype(jnp.bfloat16)
        fmat[m] = jnp.zeros_like(fmat[m])

    def compute(j, q):
        local_trade(j, q).wait()
        recv_trade(j, q).wait_recv()
        a = fac[j, q]
        total = None
        for m in range(months):
            x = jnp.concatenate([tv[j, q, m, 0], tv[j, q, m, 1]], 0)
            model = lax.dot_general(bmat[m], a, (((1,), (1,)), ((), ())),
                                    preferred_element_type=jnp.float32)
            e = (x.astype(jnp.float32) - model).astype(jnp.bfloat16)
            term = jnp.dot(bmat_t[m], e, preferred_element_type=jnp.float32)
            total = term if total is None else total + term
            fmat[m] += jnp.dot(e, a, preferred_element_type=jnp.float32)
        acc[j, q] = total

    def compute_step(s, q):
        def one(d, carry):
            jm = mirrored(d, z) - s

            @pl.when((jm >= 0) & ((s > 0) | (d == 0)))
            def _():
                compute(mirrored(d, jm), q)
            return carry
        lax.fori_loop(0, 2, one, 0)

    def rs_copy(d, j, q):
        to = z + 1 - 2 * d
        slot = jnp.where((j == to) & (d == 1), n, j)
        return pltpu.make_async_remote_copy(
            src_ref=sbuf.at[j, q], dst_ref=rbuf.at[slot, q],
            send_sem=rs_send.at[j, q], recv_sem=rs_recv.at[slot, q],
            device_id={"cuts": to}, device_id_type=MESH)

    def rs_wait(d, slot, q):
        pltpu.make_async_remote_copy(
            src_ref=sbuf.at[0, q], dst_ref=rbuf.at[slot, q],
            send_sem=rs_send.at[0, q], recv_sem=rs_recv.at[slot, q],
            device_id={"cuts": z + 1 - 2 * d}, device_id_type=MESH).wait_recv()

    def reduce_step(s, q):
        def one(d, carry):
            zm = mirrored(d, z)
            jm = s - zm

            @pl.when((jm > zm) & (jm <= n - 1))
            def _():
                j = mirrored(d, jm)

                @pl.when(zm > 0)
                def _():
                    rs_wait(d, j, q)
                    acc[j, q] = acc[j, q] + decode(rbuf.at[j, q])
                encode(sbuf.at[j, q], acc[j, q])
                rs_copy(d, j, q).start()
            return carry
        lax.fori_loop(0, 2, one, 0)

    def main_step(i, carry):
        s, q = i // n_q, i % n_q

        @pl.when(s > 0)
        def _():
            gather_step(s, q)
        compute_step(s, q)
        reduce_step(s, q)
        return carry
    lax.fori_loop(0, n * n_q, main_step, 0)

    win_t = win32.T
    window_sum = jnp.zeros((wsize, core.shape[1]), jnp.float32)
    core_sum = jnp.zeros(core.shape, jnp.float32)
    diags = []
    for m in range(months):
        drow = jnp.broadcast_to(scales[m:m + 1, :], core.shape)
        dcol = drow.T
        inner = dcol * core[...] * drow
        window_sum += lax.dot_general(fmat[m], inner, (((1,), (1,)), ((), ())),
                                      precision=HIGHEST, preferred_element_type=jnp.float32)
        gram = jnp.dot(win_t, fmat[m], precision=HIGHEST, preferred_element_type=jnp.float32)
        core_sum += dcol * gram * drow
        weighted = gram * core[...]
        by_row = jnp.sum(weighted.T * dcol, axis=0, keepdims=True)
        by_col = jnp.sum(weighted * dcol, axis=0, keepdims=True)
        diags.append(-coef * (by_row + by_col))
    wr, cr = wfin.shape[1], cfin.shape[2]
    for k in range(tiles):
        for i in range(n):
            w0, c0 = (i * tiles + k) * wr, (i * tiles + k) * cr
            part[k, i, pl.ds(0, wr), :] = -coef * window_sum[w0:w0 + wr]
            part[k, i, pl.ds(wr, cr), :] = -coef * core_sum[c0:c0 + cr]
    dbuf[t] = jnp.concatenate(
        diags + [jnp.zeros((8 - months, core.shape[1]), jnp.float32)], 0)

    def peer_t(k):
        return lax.rem(t + k, tiles)

    def peer_z(k):
        return lax.rem(z + k, n)

    def to_tile(src, dst, send, recv, k, who):
        return pltpu.make_async_remote_copy(
            src_ref=src, dst_ref=dst, send_sem=send.at[k], recv_sem=recv.at[who],
            device_id={"tile": peer_t(k)}, device_id_type=MESH)

    def to_cut(src, dst, send, recv, k, who):
        return pltpu.make_async_remote_copy(
            src_ref=src, dst_ref=dst, send_sem=send.at[k], recv_sem=recv.at[who],
            device_id={"cuts": peer_z(k)}, device_id_type=MESH)

    def p1(k, who):
        return to_tile(part.at[peer_t(k)], p1buf.at[who], p1_send, p1_recv, k, who)

    def pd(k, who):
        return to_tile(dbuf.at[who], dbuf.at[who], d_send, d_recv, k, who)

    def p2(k, who):
        return to_cut(s2.at[peer_z(k)], p2buf.at[who], p2_send, p2_recv, k, who)

    def p3(k, who):
        return to_cut(cfin.at[who, t], cfin.at[who, t], p3_send, p3_recv, k, who)

    def p4(k, who):
        return to_tile(cfin.at[:, who], cfin.at[:, who], p4_send, p4_recv, k, who)

    def p5(k, who):
        return to_tile(wfin.at[who], wfin.at[who], p5_send, p5_recv, k, who)

    for k in range(1, tiles):
        p1(k, t).start()
        pd(k, t).start()

    def small_second():
        for k in range(1, tiles):
            p1(k, peer_t(k)).wait_recv()
        total = part[t]
        for k in range(1, tiles):
            total = total + p1buf[peer_t(k)]
        s2[...] = total
        for k in range(1, n):
            p2(k, z).start()

    def small_third():
        for k in range(1, n):
            p2(k, peer_z(k)).wait_recv()
        total = s2[z]
        for k in range(1, n):
            total = total + p2buf[peer_z(k)]
        wfin[t] = total[:wr]
        cfin[z, t] = total[wr:]
        for k in range(1, n):
            p3(k, z).start()
        for k in range(1, tiles):
            p5(k, t).start()

    def small_fourth():
        for k in range(1, n):
            p3(k, peer_z(k)).wait_recv()
        for k in range(1, tiles):
            p4(k, t).start()

    def small_last():
        for k in range(1, tiles):
            p4(k, peer_t(k)).wait_recv()
            p5(k, peer_t(k)).wait_recv()
            pd(k, peer_t(k)).wait_recv()
        for k in range(tiles):
            wout_ref[pl.ds(k * wr, wr), :] = wfin[k]
            for i in range(n):
                core_ref[pl.ds((i * tiles + k) * cr, cr), :] = cfin[i, k]
        total = dbuf[0]
        for k in range(1, tiles):
            total = total + dbuf[k]
        diag_ref[...] = total[:months]
        for k in range(1, tiles):
            p1(k, t).wait_send()
            pd(k, t).wait_send()
            p4(k, t).wait_send()
            p5(k, t).wait_send()
        for k in range(1, n):
            p2(k, z).wait_send()
            p3(k, z).wait_send()

    def tail_step(i, carry):
        reduce_step(i // n_q, i % n_q)
        return carry

    stages = [small_second, small_third, small_fourth]
    for s in range(n, 2 * n - 1):
        lax.fori_loop(s * n_q, (s + 1) * n_q, tail_step, 0)
        if stages:
            stages.pop(0)()
    for stage in stages:
        stage()

    for q in range(n_q):
        @pl.when(z > 0)
        def _():
            rs_wait(0, z, q)
            acc[z, q] = acc[z, q] + decode(rbuf.at[z, q])

        @pl.when(z < n - 1)
        def _():
            rs_wait(1, n, q)
            acc[z, q] = acc[z, q] + decode(rbuf.at[n, q])
        grad_ref[pl.ds(q * r, r), :] = -coef * acc[z, q].T

    small_last()

    def drain(i, carry):
        j, q = i // n_q, i % n_q
        remote_trade(j, q).wait_send()

        @pl.when((j <= z) & (z < n - 1))
        def _():
            ag_copy(0, j, q).wait_send()

        @pl.when((j >= z) & (z > 0))
        def _():
            ag_copy(1, j, q).wait_send()

        @pl.when(j != z)
        def _():
            rs_copy(jnp.where(j > z, 0, 1), j, q).wait_send()
        return carry
    lax.fori_loop(0, n * n_q, drain, 0)

    @pl.when(t == 0)
    def _():
        for p in range(pieces):
            @pl.when(z < n - 1)
            def _():
                win_up(p).wait_send()
            for k in range(1, tiles):
                win_side(p, k).wait_send()


def fused(n, tiles, trade, factor, scales, core):
    months, rows, size = trade.shape[0], trade.shape[2], factor.shape[1]
    shard = factor.shape[0]
    r = 256
    n_q = shard // r
    wsize = 2 * rows
    pieces = wsize // r
    wr, cr = wsize // (n * tiles), size // (n * tiles)
    coef = 1.0 / math.sqrt(months * n * wsize)
    vmem = pl.BlockSpec(memory_space=pltpu.VMEM)
    anyspace = pl.BlockSpec(memory_space=pl.ANY)
    dma = pltpu.SemaphoreType.DMA
    return pl.pallas_call(
        functools.partial(kernel, n, tiles, coef),
        out_shape=(jax.ShapeDtypeStruct((shard, size), jnp.float32),
                   jax.ShapeDtypeStruct((wsize // n, size), jnp.float32),
                   jax.ShapeDtypeStruct((size, size), jnp.float32),
                   jax.ShapeDtypeStruct((months, size), jnp.float32)),
        in_specs=[anyspace, anyspace, vmem, vmem],
        out_specs=(vmem, vmem, vmem, vmem),
        scratch_shapes=[
            pltpu.VMEM((n, n_q, months, 2, rows, r), jnp.bfloat16),
            pltpu.VMEM((n, n_q, r, size), jnp.bfloat16),
            pltpu.VMEM((wsize, size), jnp.bfloat16),
            pltpu.VMEM((n, n_q, size, r), jnp.float32),
            pltpu.VMEM((n, n_q, size + 16, r), jnp.bfloat16),
            pltpu.VMEM((n + 1, n_q, size + 16, r), jnp.bfloat16),
            pltpu.VMEM((months, wsize, size), jnp.float32),
            pltpu.VMEM((months, wsize, size), jnp.bfloat16),
            pltpu.VMEM((months, size, wsize), jnp.bfloat16),
            pltpu.VMEM((tiles, n, wr + cr, size), jnp.float32),
            pltpu.VMEM((tiles, n, wr + cr, size), jnp.float32),
            pltpu.VMEM((n, wr + cr, size), jnp.float32),
            pltpu.VMEM((n, wr + cr, size), jnp.float32),
            pltpu.VMEM((n, tiles, cr, size), jnp.float32),
            pltpu.VMEM((tiles, wr, size), jnp.float32),
            pltpu.VMEM((tiles, 8, size), jnp.float32),
            dma((n, n_q)), dma((n, n_q)), dma((n, n_q)), dma((n_q,)),
            dma((2, n, n_q)), dma((n, n_q)), dma((n, n_q)), dma((n + 1, n_q)),
            dma((pieces, tiles)), dma((pieces,)),
            dma((tiles,)), dma((tiles,)), dma((n,)), dma((n,)), dma((n,)), dma((n,)),
            dma((tiles,)), dma((tiles,)), dma((tiles,)), dma((tiles,)), dma((tiles,)), dma((tiles,)),
        ],
        compiler_params=pltpu.CompilerParams(
            collective_id=0, has_side_effects=True, vmem_limit_bytes=56 * 2**20),
    )(trade, factor, scales, core)


def small_sums(n, small, wsize, size, months):
    z = lax.axis_index("cuts")
    diag = jnp.zeros((months * n, size), jnp.float32)
    diag = lax.dynamic_update_slice_in_dim(
        diag, small[wsize + size:wsize + size + months], z * months, 0)
    total = lax.psum(jnp.concatenate([small[:wsize + size], diag], 0), ("tile", "cuts"))
    window = lax.dynamic_slice_in_dim(total, z * (wsize // n), wsize // n, 0)
    diag = lax.dynamic_slice_in_dim(total, wsize + size + z * months, months, 0)
    return window, total[wsize:wsize + size], diag


def swapped(value, axis, distance):
    mask = 2**distance
    pairs = [(source, source ^ mask) for source in range(lax.axis_size(axis))]
    return lax.ppermute(value, axis, pairs)


def plain(trade, factor, scales, core):
    n = lax.axis_size("cuts")
    band_index = lax.axis_index("tile") % 2
    months, rows, size = trade.shape[0], trade.shape[2], factor.shape[1]
    wsize = 2 * rows
    own = lax.all_gather(factor, "cuts", axis=0, tiled=True)
    block = own.shape[0]
    partner = swapped(own, "tile", 0)
    columns = jnp.concatenate([jnp.where(band_index == 0, own, partner),
                               jnp.where(band_index == 0, partner, own)], 0)
    first = jnp.where(lax.axis_index("tile") == 0, own[:wsize], jnp.zeros_like(own[:wsize]))
    window = lax.psum(first, "tile")
    window32 = lax.dynamic_slice_in_dim(window, band_index * rows, rows, 0).astype(jnp.float32)
    coef = 1.0 / math.sqrt(months * n * wsize)
    acc_columns = jnp.zeros((2 * block, size), jnp.float32)
    acc_window = jnp.zeros((rows, size), jnp.float32)
    acc_core = jnp.zeros((size, size), jnp.float32)
    diags = []
    for month in range(months):
        diag_k = scales[month]
        inner = diag_k[:, None] * core * diag_k[None, :]
        mapped = jnp.dot(window32, inner, precision=HIGHEST).astype(jnp.bfloat16)
        model = lax.dot_general(mapped, columns, (((1,), (1,)), ((), ())),
                                preferred_element_type=jnp.float32)
        residual = (trade[month, 0].astype(jnp.float32) - model).astype(jnp.bfloat16)
        acc_columns = acc_columns + lax.dot_general(
            residual, mapped, (((0,), (0,)), ((), ())), preferred_element_type=jnp.float32)
        projected = jnp.dot(residual, columns, preferred_element_type=jnp.float32)
        acc_window = acc_window + jnp.dot(projected, inner.T, precision=HIGHEST)
        gram = jnp.dot(window32.T, projected, precision=HIGHEST)
        acc_core = acc_core + diag_k[:, None] * gram * diag_k[None, :]
        weighted = gram * core
        diags.append(jnp.dot(weighted, diag_k, precision=HIGHEST)
                     + jnp.dot(weighted.T, diag_k, precision=HIGHEST))
    halves = acc_columns.reshape(2, block, size)
    mine = jnp.where(band_index == 0, halves[0], halves[1])
    other = jnp.where(band_index == 0, halves[1], halves[0])
    grad = lax.psum_scatter(mine + swapped(other, "tile", 0), "cuts",
                            scatter_dimension=0, tiled=True)
    padded = lax.dynamic_update_slice_in_dim(
        jnp.zeros((wsize, size), jnp.float32), acc_window, band_index * rows, 0)
    small = jnp.concatenate([padded, acc_core, jnp.stack(diags, 0)], 0)
    window, core_total, diag = small_sums(n, -coef * small, wsize, size, months)
    return -coef * grad, window, core_total, diag


def body(trade, factor, scales, core):
    n, tiles = lax.axis_size("cuts"), lax.axis_size("tile")
    months, wsize, size = trade.shape[0], 2 * trade.shape[2], factor.shape[1]
    if factor.shape[0] % 256 or factor.shape[0] < wsize or n < 2 or months > 8:
        return plain(trade, factor, scales, core)
    if wsize % (8 * n * tiles) or size % (8 * n * tiles):
        return plain(trade, factor, scales, core)
    return fused(n, tiles, trade, factor, scales, core)


def solution(mesh):
    return jax.shard_map(
        body,
        mesh=mesh,
        in_specs=(
            P(("groups", "cuts"), "tile", None, None),
            P(("groups", "tile", "cuts"), None),
            P(("groups", "cuts"), None),
            P("groups", None),
        ),
        out_specs=(
            P(("groups", "tile", "cuts"), None),
            P(("groups", "cuts"), None),
            P("groups", None),
            P(("groups", "cuts"), None),
        ),
        check_vma=False,
    )
```

```python
import functools
import math

import jax
import jax.numpy as jnp
from jax import lax
from jax.experimental import pallas as pl
from jax.experimental.pallas import tpu as pltpu
from jax.sharding import PartitionSpec as P

HIGHEST = lax.Precision.HIGHEST
MESH = pl.DeviceIdType.MESH


SPAN = 250.0


def encode(ref, x):
    size = x.shape[0]
    top = jnp.maximum(jnp.max(jnp.abs(x), axis=0, keepdims=True), 1e-30)
    scale = (top * 1.008).astype(jnp.bfloat16).astype(jnp.float32)
    u = x * (1.0 / scale)
    a = jnp.exp2(jnp.abs(u) * SPAN - 0.5 * SPAN)
    ref[pl.ds(0, size), :] = jnp.where(u < 0.0, -a, a).astype(jnp.bfloat16)
    ref[pl.ds(size, 16), :] = jnp.broadcast_to(scale, (16, x.shape[1])).astype(jnp.bfloat16)


def decode(ref):
    size = ref.shape[0] - 16
    y = ref[pl.ds(0, size), :].astype(jnp.float32)
    scale = ref[pl.ds(size, 16), :].astype(jnp.float32)[:1]
    u = jnp.log(jnp.abs(y)) * (1.0 / (SPAN * math.log(2.0))) + 0.5
    return jnp.where(y < 0.0, -u, u) * scale


def kernel(n, tiles, coef, trade, factor, scales, core, grad_ref, wout_ref, core_ref, diag_ref,
           tv, fac, win, acc, sbuf, rbuf, fmat, bmat, bmat_t,
           part, p1buf, s2, p2buf, cfin, wfin, dbuf,
           tl_sem, ts_sem, tr_sem, own_sem, ag_send, ag_recv, rs_send, rs_recv, win_send, win_recv,
           p1_send, p1_recv, p2_send, p2_recv, p3_send, p3_recv, p4_send, p4_recv, p5_send, p5_recv,
           d_send, d_recv):
    z = lax.axis_index("cuts")
    t = lax.axis_index("tile")
    c = lax.rem(t, 2)
    partner = t + 1 - 2 * c
    months = trade.shape[0]
    rows = trade.shape[2]
    n_q, r = fac.shape[1], fac.shape[2]
    shard = n_q * r
    block = n * shard
    wsize = win.shape[0]
    pieces = win_recv.shape[0]
    wrow = wsize // pieces

    barrier = pltpu.get_barrier_semaphore()

    for k in range(1, n):
        pl.semaphore_signal(
            barrier, inc=1, device_id={"cuts": lax.rem(z + k, n)}, device_id_type=MESH)
    for k in range(1, tiles):
        pl.semaphore_signal(
            barrier, inc=1, device_id={"tile": lax.rem(t + k, tiles)}, device_id_type=MESH)

    def own_copy(q):
        return pltpu.make_async_copy(factor.at[pl.ds(q * r, r)], fac.at[z, q], own_sem.at[q])

    def local_trade(j, q):
        off = pl.multiple_of(c * block + j * shard + q * r, 128)
        return pltpu.make_async_copy(
            trade.at[:, 0, :, pl.ds(off, r)], tv.at[j, q, :, c], tl_sem.at[j, q])

    def remote_trade(j, q):
        off = pl.multiple_of((1 - c) * block + j * shard + q * r, 128)
        return pltpu.make_async_remote_copy(
            src_ref=trade.at[:, 0, :, pl.ds(off, r)], dst_ref=tv.at[j, q, :, c],
            send_sem=ts_sem.at[j, q], recv_sem=tr_sem.at[j, q],
            device_id={"tile": partner}, device_id_type=MESH)

    def recv_trade(j, q):
        off = pl.multiple_of(c * block + j * shard + q * r, 128)
        return pltpu.make_async_remote_copy(
            src_ref=trade.at[:, 0, :, pl.ds(off, r)], dst_ref=tv.at[j, q, :, 1 - c],
            send_sem=ts_sem.at[j, q], recv_sem=tr_sem.at[j, q],
            device_id={"tile": partner}, device_id_type=MESH)

    for q in range(n_q):
        own_copy(q).start()

    pl.semaphore_wait(barrier, tiles + n - 2)
    for q in range(n_q):
        own_copy(q).wait()

    def win_up(p):
        return pltpu.make_async_remote_copy(
            src_ref=win.at[pl.ds(p * wrow, wrow)], dst_ref=win.at[pl.ds(p * wrow, wrow)],
            send_sem=win_send.at[p, 0], recv_sem=win_recv.at[p],
            device_id={"cuts": z + 1}, device_id_type=MESH)

    def win_side(p, k):
        return pltpu.make_async_remote_copy(
            src_ref=win.at[pl.ds(p * wrow, wrow)], dst_ref=win.at[pl.ds(p * wrow, wrow)],
            send_sem=win_send.at[p, k], recv_sem=win_recv.at[p],
            device_id={"tile": k}, device_id_type=MESH)

    def win_recv_wait(p):
        win_up(p).wait_recv()

    @pl.when((t == 0) & (z == 0))
    def _():
        for p in range(pieces):
            win[pl.ds(p * wrow, wrow), :] = fac[0, p]

    @pl.when((t == 0) & (z == 0))
    def _():
        for p in range(pieces):
            win_up(p).start()
            for k in range(1, tiles):
                win_side(p, k).start()

    def mirrored(d, x):
        return jnp.where(d == 0, x, n - 1 - x)

    def ag_copy(d, j, q):
        return pltpu.make_async_remote_copy(
            src_ref=fac.at[j, q], dst_ref=fac.at[j, q],
            send_sem=ag_send.at[d, j, q], recv_sem=ag_recv.at[j, q],
            device_id={"cuts": z + 1 - 2 * d}, device_id_type=MESH)

    def gather_step(s, q):
        def one(d, carry):
            zm = mirrored(d, z)
            jm = zm - s

            @pl.when(jm >= 0)
            def _():
                j = mirrored(d, jm)

                @pl.when(s > 0)
                def _():
                    ag_copy(d, j, q).wait_recv()

                @pl.when(zm < n - 1)
                def _():
                    ag_copy(d, j, q).start()
            return carry
        lax.fori_loop(0, 2, one, 0)

    early = jnp.where(t >= 2, n_q, jnp.where(z > 0, n_q // 2, 0))
    for q in range(n_q):
        @pl.when(z > 0)
        def _():
            ag_copy(1, z, q).start()

        @pl.when((z < n - 1) & (q < early))
        def _():
            ag_copy(0, z, q).start()

    def trade_start(i, carry):
        s, q = i // n_q, i % n_q
        for d in (0, 1):
            zm = mirrored(d, z)

            @pl.when((zm - s >= 0) & ((s > 0) | (d == 0)))
            def _():
                j = mirrored(d, zm - s)
                local_trade(j, q).start()
                remote_trade(j, q).start()
        return carry
    lax.fori_loop(0, n * n_q, trade_start, 0)

    @pl.when((t != 0) | (z != 0))
    def _():
        for p in range(pieces):
            win_recv_wait(p)

            @pl.when(t == 0)
            def _():
                @pl.when(z < n - 1)
                def _():
                    win_up(p).start()
                for k in range(1, tiles):
                    win_side(p, k).start()

    @pl.when((t == 0) & (z == 0))
    def _():
        for p in range(pieces):
            win_up(p).wait_send()

    for q in range(n_q):
        @pl.when((z < n - 1) & (q >= early))
        def _():
            ag_copy(0, z, q).start()

    def inner_of(m):
        drow = jnp.broadcast_to(scales[m:m + 1, :], core.shape)
        return drow.T * core[...] * drow

    win32 = win[...].astype(jnp.float32)
    for m in range(months):
        mapped = jnp.dot(win32, inner_of(m), precision=HIGHEST,
                         preferred_element_type=jnp.float32)
        bmat[m] = mapped.astype(jnp.bfloat16)
        bmat_t[m] = mapped.T.astype(jnp.bfloat16)
        fmat[m] = jnp.zeros_like(fmat[m])

    def compute(j, q):
        local_trade(j, q).wait()
        recv_trade(j, q).wait_recv()
        a = fac[j, q]
        total = None
        for m in range(months):
            x = jnp.concatenate([tv[j, q, m, 0], tv[j, q, m, 1]], 0)
            model = lax.dot_general(bmat[m], a, (((1,), (1,)), ((), ())),
                                    preferred_element_type=jnp.float32)
            e = (x.astype(jnp.float32) - model).astype(jnp.bfloat16)
            term = jnp.dot(bmat_t[m], e, preferred_element_type=jnp.float32)
            total = term if total is None else total + term
            fmat[m] += jnp.dot(e, a, preferred_element_type=jnp.float32)
        acc[j, q] = total

    def compute_step(s, q):
        def one(d, carry):
            jm = mirrored(d, z) - s

            @pl.when((jm >= 0) & ((s > 0) | (d == 0)))
            def _():
                compute(mirrored(d, jm), q)
            return carry
        lax.fori_loop(0, 2, one, 0)

    def rs_copy(d, j, q):
        to = z + 1 - 2 * d
        slot = jnp.where((j == to) & (d == 1), n, j)
        return pltpu.make_async_remote_copy(
            src_ref=sbuf.at[j, q], dst_ref=rbuf.at[slot, q],
            send_sem=rs_send.at[j, q], recv_sem=rs_recv.at[slot, q],
            device_id={"cuts": to}, device_id_type=MESH)

    def rs_wait(d, slot, q):
        pltpu.make_async_remote_copy(
            src_ref=sbuf.at[0, q], dst_ref=rbuf.at[slot, q],
            send_sem=rs_send.at[0, q], recv_sem=rs_recv.at[slot, q],
            device_id={"cuts": z + 1 - 2 * d}, device_id_type=MESH).wait_recv()

    def reduce_step(s, q):
        def one(d, carry):
            zm = mirrored(d, z)
            jm = s - zm

            @pl.when((jm > zm) & (jm <= n - 1))
            def _():
                j = mirrored(d, jm)

                @pl.when(zm > 0)
                def _():
                    rs_wait(d, j, q)
                    acc[j, q] = acc[j, q] + decode(rbuf.at[j, q])
                encode(sbuf.at[j, q], acc[j, q])
                rs_copy(d, j, q).start()
            return carry
        lax.fori_loop(0, 2, one, 0)

    def main_step(i, carry):
        s, q = i // n_q, i % n_q

        @pl.when(s > 0)
        def _():
            gather_step(s, q)
        compute_step(s, q)
        reduce_step(s, q)
        return carry
    lax.fori_loop(0, n * n_q, main_step, 0)

    win_t = win32.T
    window_sum = jnp.zeros((wsize, core.shape[1]), jnp.float32)
    core_sum = jnp.zeros(core.shape, jnp.float32)
    diags = []
    for m in range(months):
        drow = jnp.broadcast_to(scales[m:m + 1, :], core.shape)
        dcol = drow.T
        inner = dcol * core[...] * drow
        window_sum += lax.dot_general(fmat[m], inner, (((1,), (1,)), ((), ())),
                                      precision=HIGHEST, preferred_element_type=jnp.float32)
        gram = jnp.dot(win_t, fmat[m], precision=HIGHEST, preferred_element_type=jnp.float32)
        core_sum += dcol * gram * drow
        weighted = gram * core[...]
        by_row = jnp.sum(weighted.T * dcol, axis=0, keepdims=True)
        by_col = jnp.sum(weighted * dcol, axis=0, keepdims=True)
        diags.append(-coef * (by_row + by_col))
    wr, cr = wfin.shape[1], cfin.shape[2]
    for k in range(tiles):
        for i in range(n):
            w0, c0 = (i * tiles + k) * wr, (i * tiles + k) * cr
            part[k, i, pl.ds(0, wr), :] = -coef * window_sum[w0:w0 + wr]
            part[k, i, pl.ds(wr, cr), :] = -coef * core_sum[c0:c0 + cr]
    dbuf[t] = jnp.concatenate(
        diags + [jnp.zeros((8 - months, core.shape[1]), jnp.float32)], 0)

    def peer_t(k):
        return lax.rem(t + k, tiles)

    def peer_z(k):
        return lax.rem(z + k, n)

    def to_tile(src, dst, send, recv, k, who):
        return pltpu.make_async_remote_copy(
            src_ref=src, dst_ref=dst, send_sem=send.at[k], recv_sem=recv.at[who],
            device_id={"tile": peer_t(k)}, device_id_type=MESH)

    def to_cut(src, dst, send, recv, k, who):
        return pltpu.make_async_remote_copy(
            src_ref=src, dst_ref=dst, send_sem=send.at[k], recv_sem=recv.at[who],
            device_id={"cuts": peer_z(k)}, device_id_type=MESH)

    def p1(k, who):
        return to_tile(part.at[peer_t(k)], p1buf.at[who], p1_send, p1_recv, k, who)

    def pd(k, who):
        return to_tile(dbuf.at[who], dbuf.at[who], d_send, d_recv, k, who)

    def p2(k, who):
        return to_cut(s2.at[peer_z(k)], p2buf.at[who], p2_send, p2_recv, k, who)

    def p3(k, who):
        return to_cut(cfin.at[who, t], cfin.at[who, t], p3_send, p3_recv, k, who)

    def p4(k, who):
        return to_tile(cfin.at[:, who], cfin.at[:, who], p4_send, p4_recv, k, who)

    def p5(k, who):
        return to_tile(wfin.at[who], wfin.at[who], p5_send, p5_recv, k, who)

    for k in range(1, tiles):
        p1(k, t).start()
        pd(k, t).start()

    def small_second():
        for k in range(1, tiles):
            p1(k, peer_t(k)).wait_recv()
        total = part[t]
        for k in range(1, tiles):
            total = total + p1buf[peer_t(k)]
        s2[...] = total
        for k in range(1, n):
            p2(k, z).start()

    def small_third():
        for k in range(1, n):
            p2(k, peer_z(k)).wait_recv()
        total = s2[z]
        for k in range(1, n):
            total = total + p2buf[peer_z(k)]
        wfin[t] = total[:wr]
        cfin[z, t] = total[wr:]
        for k in range(1, n):
            p3(k, z).start()
        for k in range(1, tiles):
            p5(k, t).start()

    def small_fourth():
        for k in range(1, n):
            p3(k, peer_z(k)).wait_recv()
        for k in range(1, tiles):
            p4(k, t).start()

    def small_last():
        for k in range(1, tiles):
            p4(k, peer_t(k)).wait_recv()
            p5(k, peer_t(k)).wait_recv()
            pd(k, peer_t(k)).wait_recv()
        for k in range(tiles):
            wout_ref[pl.ds(k * wr, wr), :] = wfin[k]
            for i in range(n):
                core_ref[pl.ds((i * tiles + k) * cr, cr), :] = cfin[i, k]
        total = dbuf[0]
        for k in range(1, tiles):
            total = total + dbuf[k]
        diag_ref[...] = total[:months]
        for k in range(1, tiles):
            p1(k, t).wait_send()
            pd(k, t).wait_send()
            p4(k, t).wait_send()
            p5(k, t).wait_send()
        for k in range(1, n):
            p2(k, z).wait_send()
            p3(k, z).wait_send()

    def tail_step(i, carry):
        reduce_step(i // n_q, i % n_q)
        return carry

    stages = [small_second, small_third, small_fourth]
    for s in range(n, 2 * n - 1):
        lax.fori_loop(s * n_q, (s + 1) * n_q, tail_step, 0)
        if stages:
            stages.pop(0)()
    for stage in stages:
        stage()

    for q in range(n_q):
        @pl.when(z > 0)
        def _():
            rs_wait(0, z, q)
            acc[z, q] = acc[z, q] + decode(rbuf.at[z, q])

        @pl.when(z < n - 1)
        def _():
            rs_wait(1, n, q)
            acc[z, q] = acc[z, q] + decode(rbuf.at[n, q])
        grad_ref[pl.ds(q * r, r), :] = -coef * acc[z, q].T

    small_last()

    def drain(i, carry):
        j, q = i // n_q, i % n_q
        remote_trade(j, q).wait_send()

        @pl.when((j <= z) & (z < n - 1))
        def _():
            ag_copy(0, j, q).wait_send()

        @pl.when((j >= z) & (z > 0))
        def _():
            ag_copy(1, j, q).wait_send()

        @pl.when(j != z)
        def _():
            rs_copy(jnp.where(j > z, 0, 1), j, q).wait_send()
        return carry
    lax.fori_loop(0, n * n_q, drain, 0)

    @pl.when(t == 0)
    def _():
        for p in range(pieces):
            @pl.when((z > 0) & (z < n - 1))
            def _():
                win_up(p).wait_send()
            for k in range(1, tiles):
                win_side(p, k).wait_send()


def fused(n, tiles, trade, factor, scales, core):
    months, rows, size = trade.shape[0], trade.shape[2], factor.shape[1]
    shard = factor.shape[0]
    r = 256
    n_q = shard // r
    wsize = 2 * rows
    pieces = wsize // r
    wr, cr = wsize // (n * tiles), size // (n * tiles)
    coef = 1.0 / math.sqrt(months * n * wsize)
    vmem = pl.BlockSpec(memory_space=pltpu.VMEM)
    anyspace = pl.BlockSpec(memory_space=pl.ANY)
    dma = pltpu.SemaphoreType.DMA
    return pl.pallas_call(
        functools.partial(kernel, n, tiles, coef),
        out_shape=(jax.ShapeDtypeStruct((shard, size), jnp.float32),
                   jax.ShapeDtypeStruct((wsize // n, size), jnp.float32),
                   jax.ShapeDtypeStruct((size, size), jnp.float32),
                   jax.ShapeDtypeStruct((months, size), jnp.float32)),
        in_specs=[anyspace, anyspace, vmem, vmem],
        out_specs=(vmem, vmem, vmem, vmem),
        scratch_shapes=[
            pltpu.VMEM((n, n_q, months, 2, rows, r), jnp.bfloat16),
            pltpu.VMEM((n, n_q, r, size), jnp.bfloat16),
            pltpu.VMEM((wsize, size), jnp.bfloat16),
            pltpu.VMEM((n, n_q, size, r), jnp.float32),
            pltpu.VMEM((n, n_q, size + 16, r), jnp.bfloat16),
            pltpu.VMEM((n + 1, n_q, size + 16, r), jnp.bfloat16),
            pltpu.VMEM((months, wsize, size), jnp.float32),
            pltpu.VMEM((months, wsize, size), jnp.bfloat16),
            pltpu.VMEM((months, size, wsize), jnp.bfloat16),
            pltpu.VMEM((tiles, n, wr + cr, size), jnp.float32),
            pltpu.VMEM((tiles, n, wr + cr, size), jnp.float32),
            pltpu.VMEM((n, wr + cr, size), jnp.float32),
            pltpu.VMEM((n, wr + cr, size), jnp.float32),
            pltpu.VMEM((n, tiles, cr, size), jnp.float32),
            pltpu.VMEM((tiles, wr, size), jnp.float32),
            pltpu.VMEM((tiles, 8, size), jnp.float32),
            dma((n, n_q)), dma((n, n_q)), dma((n, n_q)), dma((n_q,)),
            dma((2, n, n_q)), dma((n, n_q)), dma((n, n_q)), dma((n + 1, n_q)),
            dma((pieces, tiles)), dma((pieces,)),
            dma((tiles,)), dma((tiles,)), dma((n,)), dma((n,)), dma((n,)), dma((n,)),
            dma((tiles,)), dma((tiles,)), dma((tiles,)), dma((tiles,)), dma((tiles,)), dma((tiles,)),
        ],
        compiler_params=pltpu.CompilerParams(
            collective_id=0, has_side_effects=True, vmem_limit_bytes=56 * 2**20),
    )(trade, factor, scales, core)


def small_sums(n, small, wsize, size, months):
    z = lax.axis_index("cuts")
    diag = jnp.zeros((months * n, size), jnp.float32)
    diag = lax.dynamic_update_slice_in_dim(
        diag, small[wsize + size:wsize + size + months], z * months, 0)
    total = lax.psum(jnp.concatenate([small[:wsize + size], diag], 0), ("tile", "cuts"))
    window = lax.dynamic_slice_in_dim(total, z * (wsize // n), wsize // n, 0)
    diag = lax.dynamic_slice_in_dim(total, wsize + size + z * months, months, 0)
    return window, total[wsize:wsize + size], diag


def swapped(value, axis, distance):
    mask = 2**distance
    pairs = [(source, source ^ mask) for source in range(lax.axis_size(axis))]
    return lax.ppermute(value, axis, pairs)


def plain(trade, factor, scales, core):
    n = lax.axis_size("cuts")
    band_index = lax.axis_index("tile") % 2
    months, rows, size = trade.shape[0], trade.shape[2], factor.shape[1]
    wsize = 2 * rows
    own = lax.all_gather(factor, "cuts", axis=0, tiled=True)
    block = own.shape[0]
    partner = swapped(own, "tile", 0)
    columns = jnp.concatenate([jnp.where(band_index == 0, own, partner),
                               jnp.where(band_index == 0, partner, own)], 0)
    first = jnp.where(lax.axis_index("tile") == 0, own[:wsize], jnp.zeros_like(own[:wsize]))
    window = lax.psum(first, "tile")
    window32 = lax.dynamic_slice_in_dim(window, band_index * rows, rows, 0).astype(jnp.float32)
    coef = 1.0 / math.sqrt(months * n * wsize)
    acc_columns = jnp.zeros((2 * block, size), jnp.float32)
    acc_window = jnp.zeros((rows, size), jnp.float32)
    acc_core = jnp.zeros((size, size), jnp.float32)
    diags = []
    for month in range(months):
        diag_k = scales[month]
        inner = diag_k[:, None] * core * diag_k[None, :]
        mapped = jnp.dot(window32, inner, precision=HIGHEST).astype(jnp.bfloat16)
        model = lax.dot_general(mapped, columns, (((1,), (1,)), ((), ())),
                                preferred_element_type=jnp.float32)
        residual = (trade[month, 0].astype(jnp.float32) - model).astype(jnp.bfloat16)
        acc_columns = acc_columns + lax.dot_general(
            residual, mapped, (((0,), (0,)), ((), ())), preferred_element_type=jnp.float32)
        projected = jnp.dot(residual, columns, preferred_element_type=jnp.float32)
        acc_window = acc_window + jnp.dot(projected, inner.T, precision=HIGHEST)
        gram = jnp.dot(window32.T, projected, precision=HIGHEST)
        acc_core = acc_core + diag_k[:, None] * gram * diag_k[None, :]
        weighted = gram * core
        diags.append(jnp.dot(weighted, diag_k, precision=HIGHEST)
                     + jnp.dot(weighted.T, diag_k, precision=HIGHEST))
    halves = acc_columns.reshape(2, block, size)
    mine = jnp.where(band_index == 0, halves[0], halves[1])
    other = jnp.where(band_index == 0, halves[1], halves[0])
    grad = lax.psum_scatter(mine + swapped(other, "tile", 0), "cuts",
                            scatter_dimension=0, tiled=True)
    padded = lax.dynamic_update_slice_in_dim(
        jnp.zeros((wsize, size), jnp.float32), acc_window, band_index * rows, 0)
    small = jnp.concatenate([padded, acc_core, jnp.stack(diags, 0)], 0)
    window, core_total, diag = small_sums(n, -coef * small, wsize, size, months)
    return -coef * grad, window, core_total, diag


def body(trade, factor, scales, core):
    n, tiles = lax.axis_size("cuts"), lax.axis_size("tile")
    months, wsize, size = trade.shape[0], 2 * trade.shape[2], factor.shape[1]
    if factor.shape[0] % 256 or factor.shape[0] < wsize or n < 2 or months > 8:
        return plain(trade, factor, scales, core)
    if wsize % (8 * n * tiles) or size % (8 * n * tiles):
        return plain(trade, factor, scales, core)
    return fused(n, tiles, trade, factor, scales, core)


def solution(mesh):
    return jax.shard_map(
        body,
        mesh=mesh,
        in_specs=(
            P(("groups", "cuts"), "tile", None, None),
            P(("groups", "tile", "cuts"), None),
            P(("groups", "cuts"), None),
            P("groups", None),
        ),
        out_specs=(
            P(("groups", "tile", "cuts"), None),
            P(("groups", "cuts"), None),
            P("groups", None),
            P(("groups", "cuts"), None),
        ),
        check_vma=False,
    )
```

```python
import functools
import math

import jax
import jax.numpy as jnp
from jax import lax
from jax.experimental import pallas as pl
from jax.experimental.pallas import tpu as pltpu
from jax.sharding import PartitionSpec as P

HIGHEST = lax.Precision.HIGHEST
MESH = pl.DeviceIdType.MESH


SPAN = 250.0


def encode(ref, x):
    size = x.shape[0]
    top = jnp.maximum(jnp.max(jnp.abs(x), axis=0, keepdims=True), 1e-30)
    scale = (top * 1.008).astype(jnp.bfloat16).astype(jnp.float32)
    u = x * (1.0 / scale)
    a = jnp.exp2(jnp.abs(u) * SPAN - 0.5 * SPAN)
    ref[pl.ds(0, size), :] = jnp.where(u < 0.0, -a, a).astype(jnp.bfloat16)
    ref[pl.ds(size, 16), :] = jnp.broadcast_to(scale, (16, x.shape[1])).astype(jnp.bfloat16)


def decode(ref):
    size = ref.shape[0] - 16
    y = ref[pl.ds(0, size), :].astype(jnp.float32)
    scale = ref[pl.ds(size, 16), :].astype(jnp.float32)[:1]
    u = jnp.log(jnp.abs(y)) * (1.0 / (SPAN * math.log(2.0))) + 0.5
    return jnp.where(y < 0.0, -u, u) * scale


def kernel(n, tiles, coef, trade, factor, scales, core, grad_ref, wout_ref, core_ref, diag_ref,
           tv, fac, win, acc, sbuf, rbuf, fmat, bmat, bmat_t,
           part, p1buf, s2, p2buf, cfin, wfin, dbuf,
           tl_sem, ts_sem, tr_sem, own_sem, ag_send, ag_recv, rs_send, rs_recv, win_send, win_recv,
           p1_send, p1_recv, p2_send, p2_recv, p3_send, p3_recv, p4_send, p4_recv, p5_send, p5_recv,
           d_send, d_recv):
    z = lax.axis_index("cuts")
    t = lax.axis_index("tile")
    c = lax.rem(t, 2)
    partner = t + 1 - 2 * c
    months = trade.shape[0]
    rows = trade.shape[2]
    n_q, r = fac.shape[1], fac.shape[2]
    shard = n_q * r
    block = n * shard
    wsize = win.shape[0]
    pieces = win_recv.shape[0]
    wrow = wsize // pieces

    barrier = pltpu.get_barrier_semaphore()

    for k in range(1, n):
        pl.semaphore_signal(
            barrier, inc=1, device_id={"cuts": lax.rem(z + k, n)}, device_id_type=MESH)
    for k in range(1, tiles):
        pl.semaphore_signal(
            barrier, inc=1, device_id={"tile": lax.rem(t + k, tiles)}, device_id_type=MESH)

    def own_copy(q):
        return pltpu.make_async_copy(factor.at[pl.ds(q * r, r)], fac.at[z, q], own_sem.at[q])

    def local_trade(j, q):
        off = pl.multiple_of(c * block + j * shard + q * r, 128)
        return pltpu.make_async_copy(
            trade.at[:, 0, :, pl.ds(off, r)], tv.at[j, q, :, c], tl_sem.at[j, q])

    def remote_trade(j, q):
        off = pl.multiple_of((1 - c) * block + j * shard + q * r, 128)
        return pltpu.make_async_remote_copy(
            src_ref=trade.at[:, 0, :, pl.ds(off, r)], dst_ref=tv.at[j, q, :, c],
            send_sem=ts_sem.at[j, q], recv_sem=tr_sem.at[j, q],
            device_id={"tile": partner}, device_id_type=MESH)

    def recv_trade(j, q):
        off = pl.multiple_of(c * block + j * shard + q * r, 128)
        return pltpu.make_async_remote_copy(
            src_ref=trade.at[:, 0, :, pl.ds(off, r)], dst_ref=tv.at[j, q, :, 1 - c],
            send_sem=ts_sem.at[j, q], recv_sem=tr_sem.at[j, q],
            device_id={"tile": partner}, device_id_type=MESH)

    for q in range(n_q):
        own_copy(q).start()

    pl.semaphore_wait(barrier, tiles + n - 2)
    for q in range(n_q):
        own_copy(q).wait()

    def win_up(p):
        return pltpu.make_async_remote_copy(
            src_ref=win.at[pl.ds(p * wrow, wrow)], dst_ref=win.at[pl.ds(p * wrow, wrow)],
            send_sem=win_send.at[p, 0], recv_sem=win_recv.at[p],
            device_id={"cuts": z + 1}, device_id_type=MESH)

    def win_side(p, k):
        return pltpu.make_async_remote_copy(
            src_ref=win.at[pl.ds(p * wrow, wrow)], dst_ref=win.at[pl.ds(p * wrow, wrow)],
            send_sem=win_send.at[p, k], recv_sem=win_recv.at[p],
            device_id={"tile": k}, device_id_type=MESH)

    def win_recv_wait(p):
        win_up(p).wait_recv()

    @pl.when((t == 0) & (z == 0))
    def _():
        for p in range(pieces):
            win[pl.ds(p * wrow, wrow), :] = fac[0, p]

    @pl.when((t == 0) & (z == 0))
    def _():
        for p in range(pieces):
            win_up(p).start()
            for k in range(1, tiles):
                win_side(p, k).start()

    def mirrored(d, x):
        return jnp.where(d == 0, x, n - 1 - x)

    def ag_copy(d, j, q):
        return pltpu.make_async_remote_copy(
            src_ref=fac.at[j, q], dst_ref=fac.at[j, q],
            send_sem=ag_send.at[d, j, q], recv_sem=ag_recv.at[j, q],
            device_id={"cuts": z + 1 - 2 * d}, device_id_type=MESH)

    def gather_step(s, q):
        def one(d, carry):
            zm = mirrored(d, z)
            jm = zm - s

            @pl.when(jm >= 0)
            def _():
                j = mirrored(d, jm)

                @pl.when(s > 0)
                def _():
                    ag_copy(d, j, q).wait_recv()

                @pl.when(zm < n - 1)
                def _():
                    ag_copy(d, j, q).start()
            return carry
        lax.fori_loop(0, 2, one, 0)

    early = jnp.where(t >= 2, n_q, jnp.where(z > 0, n_q // 2, 0))
    for q in range(n_q):
        @pl.when(z > 0)
        def _():
            ag_copy(1, z, q).start()

        @pl.when((z < n - 1) & (q < early))
        def _():
            ag_copy(0, z, q).start()

    def trade_start(i, carry):
        s, q = i // n_q, i % n_q
        for d in (0, 1):
            zm = mirrored(d, z)

            @pl.when((zm - s >= 0) & ((s > 0) | (d == 0)))
            def _():
                j = mirrored(d, zm - s)
                local_trade(j, q).start()
                remote_trade(j, q).start()
        return carry
    lax.fori_loop(0, n * n_q, trade_start, 0)

    @pl.when((t != 0) | (z != 0))
    def _():
        for p in range(pieces):
            win_recv_wait(p)

            @pl.when(t == 0)
            def _():
                @pl.when(z < n - 1)
                def _():
                    win_up(p).start()
                for k in range(1, tiles):
                    win_side(p, k).start()

    @pl.when((t == 0) & (z == 0))
    def _():
        for p in range(pieces):
            win_up(p).wait_send()

    for q in range(n_q):
        @pl.when((z < n - 1) & (q >= early))
        def _():
            ag_copy(0, z, q).start()

    def inner_of(m):
        drow = jnp.broadcast_to(scales[m:m + 1, :], core.shape)
        return drow.T * core[...] * drow

    win32 = win[...].astype(jnp.float32)
    for m in range(months):
        mapped = jnp.dot(win32, inner_of(m), precision=HIGHEST,
                         preferred_element_type=jnp.float32)
        bmat[m] = mapped.astype(jnp.bfloat16)
        bmat_t[m] = mapped.T.astype(jnp.bfloat16)
        fmat[m] = jnp.zeros_like(fmat[m])

    def compute(j, q):
        local_trade(j, q).wait()
        recv_trade(j, q).wait_recv()
        a = fac[j, q]
        total = None
        for m in range(months):
            x = jnp.concatenate([tv[j, q, m, 0], tv[j, q, m, 1]], 0)
            model = lax.dot_general(bmat[m], a, (((1,), (1,)), ((), ())),
                                    preferred_element_type=jnp.float32)
            e = (x.astype(jnp.float32) - model).astype(jnp.bfloat16)
            term = jnp.dot(bmat_t[m], e, preferred_element_type=jnp.float32)
            total = term if total is None else total + term
            fmat[m] += jnp.dot(e, a, preferred_element_type=jnp.float32)
        acc[j, q] = total

    def compute_step(s, q):
        def one(d, carry):
            jm = mirrored(d, z) - s

            @pl.when((jm >= 0) & ((s > 0) | (d == 0)))
            def _():
                compute(mirrored(d, jm), q)
            return carry
        lax.fori_loop(0, 2, one, 0)

    def rs_copy(d, j, q):
        to = z + 1 - 2 * d
        slot = jnp.where((j == to) & (d == 1), n, j)
        return pltpu.make_async_remote_copy(
            src_ref=sbuf.at[j, q], dst_ref=rbuf.at[slot, q],
            send_sem=rs_send.at[j, q], recv_sem=rs_recv.at[slot, q],
            device_id={"cuts": to}, device_id_type=MESH)

    def rs_wait(d, slot, q):
        pltpu.make_async_remote_copy(
            src_ref=sbuf.at[0, q], dst_ref=rbuf.at[slot, q],
            send_sem=rs_send.at[0, q], recv_sem=rs_recv.at[slot, q],
            device_id={"cuts": z + 1 - 2 * d}, device_id_type=MESH).wait_recv()

    def reduce_step(s, q):
        def one(d, carry):
            zm = mirrored(d, z)
            jm = s - zm

            @pl.when((jm > zm) & (jm <= n - 1))
            def _():
                j = mirrored(d, jm)

                @pl.when(zm > 0)
                def _():
                    rs_wait(d, j, q)
                    acc[j, q] = acc[j, q] + decode(rbuf.at[j, q])
                encode(sbuf.at[j, q], acc[j, q])
                rs_copy(d, j, q).start()
            return carry
        lax.fori_loop(0, 2, one, 0)

    def main_step(i, carry):
        s, q = i // n_q, i % n_q

        @pl.when(s > 0)
        def _():
            gather_step(s, q)
        compute_step(s, q)
        reduce_step(s, q)
        return carry
    wr, cr = wfin.shape[1], cfin.shape[2]

    def peer_t(k):
        return lax.rem(t + k, tiles)

    def peer_z(k):
        return lax.rem(z + k, n)

    def to_tile(src, dst, send, recv, k, who):
        return pltpu.make_async_remote_copy(
            src_ref=src, dst_ref=dst, send_sem=send.at[k], recv_sem=recv.at[who],
            device_id={"tile": peer_t(k)}, device_id_type=MESH)

    def to_cut(src, dst, send, recv, k, who):
        return pltpu.make_async_remote_copy(
            src_ref=src, dst_ref=dst, send_sem=send.at[k], recv_sem=recv.at[who],
            device_id={"cuts": peer_z(k)}, device_id_type=MESH)

    def p1(k, who):
        return to_tile(part.at[peer_t(k)], p1buf.at[who], p1_send, p1_recv, k, who)

    def pd(k, who):
        return to_tile(dbuf.at[who], dbuf.at[who], d_send, d_recv, k, who)

    def p2(k, who):
        return to_cut(s2.at[peer_z(k)], p2buf.at[who], p2_send, p2_recv, k, who)

    def p3(k, who):
        return to_cut(cfin.at[who, t], cfin.at[who, t], p3_send, p3_recv, k, who)

    def p4(k, who):
        return to_tile(cfin.at[:, who], cfin.at[:, who], p4_send, p4_recv, k, who)

    def p5(k, who):
        return to_tile(wfin.at[who], wfin.at[who], p5_send, p5_recv, k, who)

    def finish():
        win_t = win32.T
        window_sum = jnp.zeros((wsize, core.shape[1]), jnp.float32)
        core_sum = jnp.zeros(core.shape, jnp.float32)
        diags = []
        for m in range(months):
            drow = jnp.broadcast_to(scales[m:m + 1, :], core.shape)
            dcol = drow.T
            inner = dcol * core[...] * drow
            window_sum += lax.dot_general(fmat[m], inner, (((1,), (1,)), ((), ())),
                                          precision=HIGHEST, preferred_element_type=jnp.float32)
            gram = jnp.dot(win_t, fmat[m], precision=HIGHEST, preferred_element_type=jnp.float32)
            core_sum += dcol * gram * drow
            weighted = gram * core[...]
            by_row = jnp.sum(weighted.T * dcol, axis=0, keepdims=True)
            by_col = jnp.sum(weighted * dcol, axis=0, keepdims=True)
            diags.append(-coef * (by_row + by_col))
        for k in range(tiles):
            for i in range(n):
                w0, c0 = (i * tiles + k) * wr, (i * tiles + k) * cr
                part[k, i, pl.ds(0, wr), :] = -coef * window_sum[w0:w0 + wr]
                part[k, i, pl.ds(wr, cr), :] = -coef * core_sum[c0:c0 + cr]
        dbuf[t] = jnp.concatenate(
            diags + [jnp.zeros((8 - months, core.shape[1]), jnp.float32)], 0)
        for k in range(1, tiles):
            p1(k, t).start()
            pd(k, t).start()

    done = 0
    for last in range(n // 2, n):
        lax.fori_loop(done * n_q, (last + 1) * n_q, main_step, 0)
        done = last + 1
        pl.when(jnp.maximum(z, n - 1 - z) == last)(finish)

    def small_second():
        for k in range(1, tiles):
            p1(k, peer_t(k)).wait_recv()
        total = part[t]
        for k in range(1, tiles):
            total = total + p1buf[peer_t(k)]
        s2[...] = total
        for k in range(1, n):
            p2(k, z).start()

    def small_third():
        for k in range(1, n):
            p2(k, peer_z(k)).wait_recv()
        total = s2[z]
        for k in range(1, n):
            total = total + p2buf[peer_z(k)]
        wfin[t] = total[:wr]
        cfin[z, t] = total[wr:]
        for k in range(1, n):
            p3(k, z).start()
        for k in range(1, tiles):
            p5(k, t).start()

    def small_fourth():
        for k in range(1, n):
            p3(k, peer_z(k)).wait_recv()
        for k in range(1, tiles):
            p4(k, t).start()

    def small_last():
        for k in range(1, tiles):
            p4(k, peer_t(k)).wait_recv()
            p5(k, peer_t(k)).wait_recv()
            pd(k, peer_t(k)).wait_recv()
        for k in range(tiles):
            wout_ref[pl.ds(k * wr, wr), :] = wfin[k]
            for i in range(n):
                core_ref[pl.ds((i * tiles + k) * cr, cr), :] = cfin[i, k]
        total = dbuf[0]
        for k in range(1, tiles):
            total = total + dbuf[k]
        diag_ref[...] = total[:months]
        for k in range(1, tiles):
            p1(k, t).wait_send()
            pd(k, t).wait_send()
            p4(k, t).wait_send()
            p5(k, t).wait_send()
        for k in range(1, n):
            p2(k, z).wait_send()
            p3(k, z).wait_send()

    def tail_step(i, carry):
        reduce_step(i // n_q, i % n_q)
        return carry

    stages = [small_second, small_third, small_fourth]
    for s in range(n, 2 * n - 1):
        lax.fori_loop(s * n_q, (s + 1) * n_q, tail_step, 0)
        if stages:
            stages.pop(0)()
    for stage in stages:
        stage()

    for q in range(n_q):
        @pl.when(z > 0)
        def _():
            rs_wait(0, z, q)
            acc[z, q] = acc[z, q] + decode(rbuf.at[z, q])

        @pl.when(z < n - 1)
        def _():
            rs_wait(1, n, q)
            acc[z, q] = acc[z, q] + decode(rbuf.at[n, q])
        grad_ref[pl.ds(q * r, r), :] = -coef * acc[z, q].T

    small_last()

    def drain(i, carry):
        j, q = i // n_q, i % n_q
        remote_trade(j, q).wait_send()

        @pl.when((j <= z) & (z < n - 1))
        def _():
            ag_copy(0, j, q).wait_send()

        @pl.when((j >= z) & (z > 0))
        def _():
            ag_copy(1, j, q).wait_send()

        @pl.when(j != z)
        def _():
            rs_copy(jnp.where(j > z, 0, 1), j, q).wait_send()
        return carry
    lax.fori_loop(0, n * n_q, drain, 0)

    @pl.when(t == 0)
    def _():
        for p in range(pieces):
            @pl.when((z > 0) & (z < n - 1))
            def _():
                win_up(p).wait_send()
            for k in range(1, tiles):
                win_side(p, k).wait_send()


def fused(n, tiles, trade, factor, scales, core):
    months, rows, size = trade.shape[0], trade.shape[2], factor.shape[1]
    shard = factor.shape[0]
    r = 256
    n_q = shard // r
    wsize = 2 * rows
    pieces = wsize // r
    wr, cr = wsize // (n * tiles), size // (n * tiles)
    coef = 1.0 / math.sqrt(months * n * wsize)
    vmem = pl.BlockSpec(memory_space=pltpu.VMEM)
    anyspace = pl.BlockSpec(memory_space=pl.ANY)
    dma = pltpu.SemaphoreType.DMA
    return pl.pallas_call(
        functools.partial(kernel, n, tiles, coef),
        out_shape=(jax.ShapeDtypeStruct((shard, size), jnp.float32),
                   jax.ShapeDtypeStruct((wsize // n, size), jnp.float32),
                   jax.ShapeDtypeStruct((size, size), jnp.float32),
                   jax.ShapeDtypeStruct((months, size), jnp.float32)),
        in_specs=[anyspace, anyspace, vmem, vmem],
        out_specs=(vmem, vmem, vmem, vmem),
        scratch_shapes=[
            pltpu.VMEM((n, n_q, months, 2, rows, r), jnp.bfloat16),
            pltpu.VMEM((n, n_q, r, size), jnp.bfloat16),
            pltpu.VMEM((wsize, size), jnp.bfloat16),
            pltpu.VMEM((n, n_q, size, r), jnp.float32),
            pltpu.VMEM((n, n_q, size + 16, r), jnp.bfloat16),
            pltpu.VMEM((n + 1, n_q, size + 16, r), jnp.bfloat16),
            pltpu.VMEM((months, wsize, size), jnp.float32),
            pltpu.VMEM((months, wsize, size), jnp.bfloat16),
            pltpu.VMEM((months, size, wsize), jnp.bfloat16),
            pltpu.VMEM((tiles, n, wr + cr, size), jnp.float32),
            pltpu.VMEM((tiles, n, wr + cr, size), jnp.float32),
            pltpu.VMEM((n, wr + cr, size), jnp.float32),
            pltpu.VMEM((n, wr + cr, size), jnp.float32),
            pltpu.VMEM((n, tiles, cr, size), jnp.float32),
            pltpu.VMEM((tiles, wr, size), jnp.float32),
            pltpu.VMEM((tiles, 8, size), jnp.float32),
            dma((n, n_q)), dma((n, n_q)), dma((n, n_q)), dma((n_q,)),
            dma((2, n, n_q)), dma((n, n_q)), dma((n, n_q)), dma((n + 1, n_q)),
            dma((pieces, tiles)), dma((pieces,)),
            dma((tiles,)), dma((tiles,)), dma((n,)), dma((n,)), dma((n,)), dma((n,)),
            dma((tiles,)), dma((tiles,)), dma((tiles,)), dma((tiles,)), dma((tiles,)), dma((tiles,)),
        ],
        compiler_params=pltpu.CompilerParams(
            collective_id=0, has_side_effects=True, vmem_limit_bytes=56 * 2**20),
    )(trade, factor, scales, core)


def small_sums(n, small, wsize, size, months):
    z = lax.axis_index("cuts")
    diag = jnp.zeros((months * n, size), jnp.float32)
    diag = lax.dynamic_update_slice_in_dim(
        diag, small[wsize + size:wsize + size + months], z * months, 0)
    total = lax.psum(jnp.concatenate([small[:wsize + size], diag], 0), ("tile", "cuts"))
    window = lax.dynamic_slice_in_dim(total, z * (wsize // n), wsize // n, 0)
    diag = lax.dynamic_slice_in_dim(total, wsize + size + z * months, months, 0)
    return window, total[wsize:wsize + size], diag


def swapped(value, axis, distance):
    mask = 2**distance
    pairs = [(source, source ^ mask) for source in range(lax.axis_size(axis))]
    return lax.ppermute(value, axis, pairs)


def plain(trade, factor, scales, core):
    n = lax.axis_size("cuts")
    band_index = lax.axis_index("tile") % 2
    months, rows, size = trade.shape[0], trade.shape[2], factor.shape[1]
    wsize = 2 * rows
    own = lax.all_gather(factor, "cuts", axis=0, tiled=True)
    block = own.shape[0]
    partner = swapped(own, "tile", 0)
    columns = jnp.concatenate([jnp.where(band_index == 0, own, partner),
                               jnp.where(band_index == 0, partner, own)], 0)
    first = jnp.where(lax.axis_index("tile") == 0, own[:wsize], jnp.zeros_like(own[:wsize]))
    window = lax.psum(first, "tile")
    window32 = lax.dynamic_slice_in_dim(window, band_index * rows, rows, 0).astype(jnp.float32)
    coef = 1.0 / math.sqrt(months * n * wsize)
    acc_columns = jnp.zeros((2 * block, size), jnp.float32)
    acc_window = jnp.zeros((rows, size), jnp.float32)
    acc_core = jnp.zeros((size, size), jnp.float32)
    diags = []
    for month in range(months):
        diag_k = scales[month]
        inner = diag_k[:, None] * core * diag_k[None, :]
        mapped = jnp.dot(window32, inner, precision=HIGHEST).astype(jnp.bfloat16)
        model = lax.dot_general(mapped, columns, (((1,), (1,)), ((), ())),
                                preferred_element_type=jnp.float32)
        residual = (trade[month, 0].astype(jnp.float32) - model).astype(jnp.bfloat16)
        acc_columns = acc_columns + lax.dot_general(
            residual, mapped, (((0,), (0,)), ((), ())), preferred_element_type=jnp.float32)
        projected = jnp.dot(residual, columns, preferred_element_type=jnp.float32)
        acc_window = acc_window + jnp.dot(projected, inner.T, precision=HIGHEST)
        gram = jnp.dot(window32.T, projected, precision=HIGHEST)
        acc_core = acc_core + diag_k[:, None] * gram * diag_k[None, :]
        weighted = gram * core
        diags.append(jnp.dot(weighted, diag_k, precision=HIGHEST)
                     + jnp.dot(weighted.T, diag_k, precision=HIGHEST))
    halves = acc_columns.reshape(2, block, size)
    mine = jnp.where(band_index == 0, halves[0], halves[1])
    other = jnp.where(band_index == 0, halves[1], halves[0])
    grad = lax.psum_scatter(mine + swapped(other, "tile", 0), "cuts",
                            scatter_dimension=0, tiled=True)
    padded = lax.dynamic_update_slice_in_dim(
        jnp.zeros((wsize, size), jnp.float32), acc_window, band_index * rows, 0)
    small = jnp.concatenate([padded, acc_core, jnp.stack(diags, 0)], 0)
    window, core_total, diag = small_sums(n, -coef * small, wsize, size, months)
    return -coef * grad, window, core_total, diag


def body(trade, factor, scales, core):
    n, tiles = lax.axis_size("cuts"), lax.axis_size("tile")
    months, wsize, size = trade.shape[0], 2 * trade.shape[2], factor.shape[1]
    if factor.shape[0] % 256 or factor.shape[0] < wsize or n < 2 or months > 8:
        return plain(trade, factor, scales, core)
    if wsize % (8 * n * tiles) or size % (8 * n * tiles):
        return plain(trade, factor, scales, core)
    return fused(n, tiles, trade, factor, scales, core)


def solution(mesh):
    return jax.shard_map(
        body,
        mesh=mesh,
        in_specs=(
            P(("groups", "cuts"), "tile", None, None),
            P(("groups", "tile", "cuts"), None),
            P(("groups", "cuts"), None),
            P("groups", None),
        ),
        out_specs=(
            P(("groups", "tile", "cuts"), None),
            P(("groups", "cuts"), None),
            P("groups", None),
            P(("groups", "cuts"), None),
        ),
        check_vma=False,
    )
```

```python
import functools
import math

import jax
import jax.numpy as jnp
from jax import lax
from jax.experimental import pallas as pl
from jax.experimental.pallas import tpu as pltpu
from jax.sharding import PartitionSpec as P

HIGHEST = lax.Precision.HIGHEST
MESH = pl.DeviceIdType.MESH


SPAN = 250.0


def encode(ref, x):
    size = x.shape[0]
    top = jnp.maximum(jnp.max(jnp.abs(x), axis=0, keepdims=True), 1e-30)
    scale = (top * 1.008).astype(jnp.bfloat16).astype(jnp.float32)
    u = x * (1.0 / scale)
    a = jnp.exp2(jnp.abs(u) * SPAN - 0.5 * SPAN)
    ref[pl.ds(0, size), :] = jnp.where(u < 0.0, -a, a).astype(jnp.bfloat16)
    ref[pl.ds(size, 16), :] = jnp.broadcast_to(scale, (16, x.shape[1])).astype(jnp.bfloat16)


def decode(ref):
    size = ref.shape[0] - 16
    y = ref[pl.ds(0, size), :].astype(jnp.float32)
    scale = ref[pl.ds(size, 16), :].astype(jnp.float32)[:1]
    u = jnp.log(jnp.abs(y)) * (1.0 / (SPAN * math.log(2.0))) + 0.5
    return jnp.where(y < 0.0, -u, u) * scale


def kernel(n, tiles, coef, trade, factor, scales, core, grad_ref, wout_ref, core_ref, diag_ref,
           tv, fac, win, acc, sbuf, rbuf, fmat, bmat, bmat_t,
           part, p1buf, s2, p2buf, cfin, wfin, dbuf,
           tl_sem, ts_sem, tr_sem, own_sem, ag_send, ag_recv, rs_send, rs_recv, win_send, win_recv,
           p1_send, p1_recv, p2_send, p2_recv, p3_send, p3_recv, p4_send, p4_recv, p5_send, p5_recv,
           d_send, d_recv):
    z = lax.axis_index("cuts")
    t = lax.axis_index("tile")
    c = lax.rem(t, 2)
    partner = t + 1 - 2 * c
    months = trade.shape[0]
    rows = trade.shape[2]
    n_q, r = fac.shape[1], fac.shape[2]
    shard = n_q * r
    block = n * shard
    wsize = win.shape[0]
    pieces = win_recv.shape[0]
    wrow = wsize // pieces

    barrier = pltpu.get_barrier_semaphore()

    for k in range(1, n):
        pl.semaphore_signal(
            barrier, inc=1, device_id={"cuts": lax.rem(z + k, n)}, device_id_type=MESH)
    for k in range(1, tiles):
        pl.semaphore_signal(
            barrier, inc=1, device_id={"tile": lax.rem(t + k, tiles)}, device_id_type=MESH)

    def own_copy(q):
        return pltpu.make_async_copy(factor.at[pl.ds(q * r, r)], fac.at[z, q], own_sem.at[q])

    def local_trade(j, q):
        off = pl.multiple_of(c * block + j * shard + q * r, 128)
        return pltpu.make_async_copy(
            trade.at[:, 0, :, pl.ds(off, r)], tv.at[j, q, :, c], tl_sem.at[j, q])

    def remote_trade(j, q):
        off = pl.multiple_of((1 - c) * block + j * shard + q * r, 128)
        return pltpu.make_async_remote_copy(
            src_ref=trade.at[:, 0, :, pl.ds(off, r)], dst_ref=tv.at[j, q, :, c],
            send_sem=ts_sem.at[j, q], recv_sem=tr_sem.at[j, q],
            device_id={"tile": partner}, device_id_type=MESH)

    def recv_trade(j, q):
        off = pl.multiple_of(c * block + j * shard + q * r, 128)
        return pltpu.make_async_remote_copy(
            src_ref=trade.at[:, 0, :, pl.ds(off, r)], dst_ref=tv.at[j, q, :, 1 - c],
            send_sem=ts_sem.at[j, q], recv_sem=tr_sem.at[j, q],
            device_id={"tile": partner}, device_id_type=MESH)

    for q in range(n_q):
        own_copy(q).start()

    pl.semaphore_wait(barrier, tiles + n - 2)
    for q in range(n_q):
        own_copy(q).wait()

    def win_up(p):
        return pltpu.make_async_remote_copy(
            src_ref=win.at[pl.ds(p * wrow, wrow)], dst_ref=win.at[pl.ds(p * wrow, wrow)],
            send_sem=win_send.at[p, 0], recv_sem=win_recv.at[p],
            device_id={"cuts": z + 1}, device_id_type=MESH)

    def win_side(p, k):
        return pltpu.make_async_remote_copy(
            src_ref=win.at[pl.ds(p * wrow, wrow)], dst_ref=win.at[pl.ds(p * wrow, wrow)],
            send_sem=win_send.at[p, k], recv_sem=win_recv.at[p],
            device_id={"tile": k}, device_id_type=MESH)

    def win_recv_wait(p):
        win_up(p).wait_recv()

    @pl.when((t == 0) & (z == 0))
    def _():
        for p in range(pieces):
            win[pl.ds(p * wrow, wrow), :] = fac[0, p * wrow // r, pl.ds(p * wrow % r, wrow), :]

    @pl.when((t == 0) & (z == 0))
    def _():
        for p in range(pieces):
            win_up(p).start()
            for k in range(1, tiles):
                win_side(p, k).start()

    def mirrored(d, x):
        return jnp.where(d == 0, x, n - 1 - x)

    def ag_copy(d, j, q):
        return pltpu.make_async_remote_copy(
            src_ref=fac.at[j, q], dst_ref=fac.at[j, q],
            send_sem=ag_send.at[d, j, q], recv_sem=ag_recv.at[j, q],
            device_id={"cuts": z + 1 - 2 * d}, device_id_type=MESH)

    def gather_step(s, q):
        def one(d, carry):
            zm = mirrored(d, z)
            jm = zm - s

            @pl.when(jm >= 0)
            def _():
                j = mirrored(d, jm)

                @pl.when(s > 0)
                def _():
                    ag_copy(d, j, q).wait_recv()

                @pl.when(zm < n - 1)
                def _():
                    ag_copy(d, j, q).start()
            return carry
        lax.fori_loop(0, 2, one, 0)

    early = jnp.where(t >= 2, n_q, jnp.where(z > 0, n_q // 2, 0))
    for q in range(n_q):
        @pl.when(z > 0)
        def _():
            ag_copy(1, z, q).start()

        @pl.when((z < n - 1) & (q < early))
        def _():
            ag_copy(0, z, q).start()

    def trade_start(i, carry):
        s, q = i // n_q, i % n_q
        for d in (0, 1):
            zm = mirrored(d, z)

            @pl.when((zm - s >= 0) & ((s > 0) | (d == 0)))
            def _():
                j = mirrored(d, zm - s)
                local_trade(j, q).start()
                remote_trade(j, q).start()
        return carry
    lax.fori_loop(0, n * n_q, trade_start, 0)

    @pl.when((t != 0) | (z != 0))
    def _():
        for p in range(pieces):
            win_recv_wait(p)

            @pl.when(t == 0)
            def _():
                @pl.when(z < n - 1)
                def _():
                    win_up(p).start()
                for k in range(1, tiles):
                    win_side(p, k).start()

    @pl.when((t == 0) & (z == 0))
    def _():
        for p in range(pieces):
            win_up(p).wait_send()

    for q in range(n_q):
        @pl.when((z < n - 1) & (q >= early))
        def _():
            ag_copy(0, z, q).start()

    def inner_of(m):
        drow = jnp.broadcast_to(scales[m:m + 1, :], core.shape)
        return drow.T * core[...] * drow

    win32 = win[...].astype(jnp.float32)
    for m in range(months):
        mapped = jnp.dot(win32, inner_of(m), precision=HIGHEST,
                         preferred_element_type=jnp.float32)
        bmat[m] = mapped.astype(jnp.bfloat16)
        bmat_t[m] = mapped.T.astype(jnp.bfloat16)
        fmat[m] = jnp.zeros_like(fmat[m])

    def compute(j, q):
        local_trade(j, q).wait()
        recv_trade(j, q).wait_recv()
        a = fac[j, q]
        total = None
        for m in range(months):
            x = jnp.concatenate([tv[j, q, m, 0], tv[j, q, m, 1]], 0)
            model = lax.dot_general(bmat[m], a, (((1,), (1,)), ((), ())),
                                    preferred_element_type=jnp.float32)
            e = (x.astype(jnp.float32) - model).astype(jnp.bfloat16)
            term = jnp.dot(bmat_t[m], e, preferred_element_type=jnp.float32)
            total = term if total is None else total + term
            fmat[m] += jnp.dot(e, a, preferred_element_type=jnp.float32)
        acc[j, q] = total

    def compute_step(s, q):
        def one(d, carry):
            jm = mirrored(d, z) - s

            @pl.when((jm >= 0) & ((s > 0) | (d == 0)))
            def _():
                compute(mirrored(d, jm), q)
            return carry
        lax.fori_loop(0, 2, one, 0)

    def rs_copy(d, j, q):
        to = z + 1 - 2 * d
        slot = jnp.where((j == to) & (d == 1), n, j)
        return pltpu.make_async_remote_copy(
            src_ref=sbuf.at[j, q], dst_ref=rbuf.at[slot, q],
            send_sem=rs_send.at[j, q], recv_sem=rs_recv.at[slot, q],
            device_id={"cuts": to}, device_id_type=MESH)

    def rs_wait(d, slot, q):
        pltpu.make_async_remote_copy(
            src_ref=sbuf.at[0, q], dst_ref=rbuf.at[slot, q],
            send_sem=rs_send.at[0, q], recv_sem=rs_recv.at[slot, q],
            device_id={"cuts": z + 1 - 2 * d}, device_id_type=MESH).wait_recv()

    def reduce_step(s, q):
        def one(d, carry):
            zm = mirrored(d, z)
            jm = s - zm

            @pl.when((jm > zm) & (jm <= n - 1))
            def _():
                j = mirrored(d, jm)

                @pl.when(zm > 0)
                def _():
                    rs_wait(d, j, q)
                    acc[j, q] = acc[j, q] + decode(rbuf.at[j, q])
                encode(sbuf.at[j, q], acc[j, q])
                rs_copy(d, j, q).start()
            return carry
        lax.fori_loop(0, 2, one, 0)

    def main_step(i, carry):
        s, q = i // n_q, i % n_q

        @pl.when(s > 0)
        def _():
            gather_step(s, q)
        compute_step(s, q)
        reduce_step(s, q)
        return carry
    lax.fori_loop(0, n * n_q, main_step, 0)

    win_t = win32.T
    window_sum = jnp.zeros((wsize, core.shape[1]), jnp.float32)
    core_sum = jnp.zeros(core.shape, jnp.float32)
    diags = []
    for m in range(months):
        drow = jnp.broadcast_to(scales[m:m + 1, :], core.shape)
        dcol = drow.T
        inner = dcol * core[...] * drow
        window_sum += lax.dot_general(fmat[m], inner, (((1,), (1,)), ((), ())),
                                      precision=HIGHEST, preferred_element_type=jnp.float32)
        gram = jnp.dot(win_t, fmat[m], precision=HIGHEST, preferred_element_type=jnp.float32)
        core_sum += dcol * gram * drow
        weighted = gram * core[...]
        by_row = jnp.sum(weighted.T * dcol, axis=0, keepdims=True)
        by_col = jnp.sum(weighted * dcol, axis=0, keepdims=True)
        diags.append(-coef * (by_row + by_col))
    wr, cr = wfin.shape[1], cfin.shape[2]
    for k in range(tiles):
        for i in range(n):
            w0, c0 = (i * tiles + k) * wr, (i * tiles + k) * cr
            part[k, i, pl.ds(0, wr), :] = -coef * window_sum[w0:w0 + wr]
            part[k, i, pl.ds(wr, cr), :] = -coef * core_sum[c0:c0 + cr]
    dbuf[t] = jnp.concatenate(
        diags + [jnp.zeros((8 - months, core.shape[1]), jnp.float32)], 0)

    def peer_t(k):
        return lax.rem(t + k, tiles)

    def peer_z(k):
        return lax.rem(z + k, n)

    def to_tile(src, dst, send, recv, k, who):
        return pltpu.make_async_remote_copy(
            src_ref=src, dst_ref=dst, send_sem=send.at[k], recv_sem=recv.at[who],
            device_id={"tile": peer_t(k)}, device_id_type=MESH)

    def to_cut(src, dst, send, recv, k, who):
        return pltpu.make_async_remote_copy(
            src_ref=src, dst_ref=dst, send_sem=send.at[k], recv_sem=recv.at[who],
            device_id={"cuts": peer_z(k)}, device_id_type=MESH)

    def p1(k, who):
        return to_tile(part.at[peer_t(k)], p1buf.at[who], p1_send, p1_recv, k, who)

    def pd(k, who):
        return to_tile(dbuf.at[who], dbuf.at[who], d_send, d_recv, k, who)

    def p2(k, who):
        return to_cut(s2.at[peer_z(k)], p2buf.at[who], p2_send, p2_recv, k, who)

    def p3(k, who):
        return to_cut(cfin.at[who, t], cfin.at[who, t], p3_send, p3_recv, k, who)

    def p4(k, who):
        return to_tile(cfin.at[:, who], cfin.at[:, who], p4_send, p4_recv, k, who)

    def p5(k, who):
        return to_tile(wfin.at[who], wfin.at[who], p5_send, p5_recv, k, who)

    for k in range(1, tiles):
        p1(k, t).start()
        pd(k, t).start()

    def small_second():
        for k in range(1, tiles):
            p1(k, peer_t(k)).wait_recv()
        total = part[t]
        for k in range(1, tiles):
            total = total + p1buf[peer_t(k)]
        s2[...] = total
        for k in range(1, n):
            p2(k, z).start()

    def small_third():
        for k in range(1, n):
            p2(k, peer_z(k)).wait_recv()
        total = s2[z]
        for k in range(1, n):
            total = total + p2buf[peer_z(k)]
        wfin[t] = total[:wr]
        cfin[z, t] = total[wr:]
        for k in range(1, n):
            p3(k, z).start()
        for k in range(1, tiles):
            p5(k, t).start()

    def small_fourth():
        for k in range(1, n):
            p3(k, peer_z(k)).wait_recv()
        for k in range(1, tiles):
            p4(k, t).start()

    def small_last():
        for k in range(1, tiles):
            p4(k, peer_t(k)).wait_recv()
            p5(k, peer_t(k)).wait_recv()
            pd(k, peer_t(k)).wait_recv()
        for k in range(tiles):
            wout_ref[pl.ds(k * wr, wr), :] = wfin[k]
            for i in range(n):
                core_ref[pl.ds((i * tiles + k) * cr, cr), :] = cfin[i, k]
        total = dbuf[0]
        for k in range(1, tiles):
            total = total + dbuf[k]
        diag_ref[...] = total[:months]
        for k in range(1, tiles):
            p1(k, t).wait_send()
            pd(k, t).wait_send()
            p4(k, t).wait_send()
            p5(k, t).wait_send()
        for k in range(1, n):
            p2(k, z).wait_send()
            p3(k, z).wait_send()

    def tail_step(i, carry):
        reduce_step(i // n_q, i % n_q)
        return carry

    stages = [small_second, small_third, small_fourth]
    for s in range(n, 2 * n - 1):
        lax.fori_loop(s * n_q, (s + 1) * n_q, tail_step, 0)
        if stages:
            stages.pop(0)()
    for stage in stages:
        stage()

    for q in range(n_q):
        @pl.when(z > 0)
        def _():
            rs_wait(0, z, q)
            acc[z, q] = acc[z, q] + decode(rbuf.at[z, q])

        @pl.when(z < n - 1)
        def _():
            rs_wait(1, n, q)
            acc[z, q] = acc[z, q] + decode(rbuf.at[n, q])
        grad_ref[pl.ds(q * r, r), :] = -coef * acc[z, q].T

    small_last()

    def drain(i, carry):
        j, q = i // n_q, i % n_q
        remote_trade(j, q).wait_send()

        @pl.when((j <= z) & (z < n - 1))
        def _():
            ag_copy(0, j, q).wait_send()

        @pl.when((j >= z) & (z > 0))
        def _():
            ag_copy(1, j, q).wait_send()

        @pl.when(j != z)
        def _():
            rs_copy(jnp.where(j > z, 0, 1), j, q).wait_send()
        return carry
    lax.fori_loop(0, n * n_q, drain, 0)

    @pl.when(t == 0)
    def _():
        for p in range(pieces):
            @pl.when((z > 0) & (z < n - 1))
            def _():
                win_up(p).wait_send()
            for k in range(1, tiles):
                win_side(p, k).wait_send()


def fused(n, tiles, trade, factor, scales, core):
    months, rows, size = trade.shape[0], trade.shape[2], factor.shape[1]
    shard = factor.shape[0]
    r = 256
    n_q = shard // r
    wsize = 2 * rows
    pieces = wsize // 128
    wr, cr = wsize // (n * tiles), size // (n * tiles)
    coef = 1.0 / math.sqrt(months * n * wsize)
    vmem = pl.BlockSpec(memory_space=pltpu.VMEM)
    anyspace = pl.BlockSpec(memory_space=pl.ANY)
    dma = pltpu.SemaphoreType.DMA
    return pl.pallas_call(
        functools.partial(kernel, n, tiles, coef),
        out_shape=(jax.ShapeDtypeStruct((shard, size), jnp.float32),
                   jax.ShapeDtypeStruct((wsize // n, size), jnp.float32),
                   jax.ShapeDtypeStruct((size, size), jnp.float32),
                   jax.ShapeDtypeStruct((months, size), jnp.float32)),
        in_specs=[anyspace, anyspace, vmem, vmem],
        out_specs=(vmem, vmem, vmem, vmem),
        scratch_shapes=[
            pltpu.VMEM((n, n_q, months, 2, rows, r), jnp.bfloat16),
            pltpu.VMEM((n, n_q, r, size), jnp.bfloat16),
            pltpu.VMEM((wsize, size), jnp.bfloat16),
            pltpu.VMEM((n, n_q, size, r), jnp.float32),
            pltpu.VMEM((n, n_q, size + 16, r), jnp.bfloat16),
            pltpu.VMEM((n + 1, n_q, size + 16, r), jnp.bfloat16),
            pltpu.VMEM((months, wsize, size), jnp.float32),
            pltpu.VMEM((months, wsize, size), jnp.bfloat16),
            pltpu.VMEM((months, size, wsize), jnp.bfloat16),
            pltpu.VMEM((tiles, n, wr + cr, size), jnp.float32),
            pltpu.VMEM((tiles, n, wr + cr, size), jnp.float32),
            pltpu.VMEM((n, wr + cr, size), jnp.float32),
            pltpu.VMEM((n, wr + cr, size), jnp.float32),
            pltpu.VMEM((n, tiles, cr, size), jnp.float32),
            pltpu.VMEM((tiles, wr, size), jnp.float32),
            pltpu.VMEM((tiles, 8, size), jnp.float32),
            dma((n, n_q)), dma((n, n_q)), dma((n, n_q)), dma((n_q,)),
            dma((2, n, n_q)), dma((n, n_q)), dma((n, n_q)), dma((n + 1, n_q)),
            dma((pieces, tiles)), dma((pieces,)),
            dma((tiles,)), dma((tiles,)), dma((n,)), dma((n,)), dma((n,)), dma((n,)),
            dma((tiles,)), dma((tiles,)), dma((tiles,)), dma((tiles,)), dma((tiles,)), dma((tiles,)),
        ],
        compiler_params=pltpu.CompilerParams(
            collective_id=0, has_side_effects=True, vmem_limit_bytes=56 * 2**20),
    )(trade, factor, scales, core)


def small_sums(n, small, wsize, size, months):
    z = lax.axis_index("cuts")
    diag = jnp.zeros((months * n, size), jnp.float32)
    diag = lax.dynamic_update_slice_in_dim(
        diag, small[wsize + size:wsize + size + months], z * months, 0)
    total = lax.psum(jnp.concatenate([small[:wsize + size], diag], 0), ("tile", "cuts"))
    window = lax.dynamic_slice_in_dim(total, z * (wsize // n), wsize // n, 0)
    diag = lax.dynamic_slice_in_dim(total, wsize + size + z * months, months, 0)
    return window, total[wsize:wsize + size], diag


def swapped(value, axis, distance):
    mask = 2**distance
    pairs = [(source, source ^ mask) for source in range(lax.axis_size(axis))]
    return lax.ppermute(value, axis, pairs)


def plain(trade, factor, scales, core):
    n = lax.axis_size("cuts")
    band_index = lax.axis_index("tile") % 2
    months, rows, size = trade.shape[0], trade.shape[2], factor.shape[1]
    wsize = 2 * rows
    own = lax.all_gather(factor, "cuts", axis=0, tiled=True)
    block = own.shape[0]
    partner = swapped(own, "tile", 0)
    columns = jnp.concatenate([jnp.where(band_index == 0, own, partner),
                               jnp.where(band_index == 0, partner, own)], 0)
    first = jnp.where(lax.axis_index("tile") == 0, own[:wsize], jnp.zeros_like(own[:wsize]))
    window = lax.psum(first, "tile")
    window32 = lax.dynamic_slice_in_dim(window, band_index * rows, rows, 0).astype(jnp.float32)
    coef = 1.0 / math.sqrt(months * n * wsize)
    acc_columns = jnp.zeros((2 * block, size), jnp.float32)
    acc_window = jnp.zeros((rows, size), jnp.float32)
    acc_core = jnp.zeros((size, size), jnp.float32)
    diags = []
    for month in range(months):
        diag_k = scales[month]
        inner = diag_k[:, None] * core * diag_k[None, :]
        mapped = jnp.dot(window32, inner, precision=HIGHEST).astype(jnp.bfloat16)
        model = lax.dot_general(mapped, columns, (((1,), (1,)), ((), ())),
                                preferred_element_type=jnp.float32)
        residual = (trade[month, 0].astype(jnp.float32) - model).astype(jnp.bfloat16)
        acc_columns = acc_columns + lax.dot_general(
            residual, mapped, (((0,), (0,)), ((), ())), preferred_element_type=jnp.float32)
        projected = jnp.dot(residual, columns, preferred_element_type=jnp.float32)
        acc_window = acc_window + jnp.dot(projected, inner.T, precision=HIGHEST)
        gram = jnp.dot(window32.T, projected, precision=HIGHEST)
        acc_core = acc_core + diag_k[:, None] * gram * diag_k[None, :]
        weighted = gram * core
        diags.append(jnp.dot(weighted, diag_k, precision=HIGHEST)
                     + jnp.dot(weighted.T, diag_k, precision=HIGHEST))
    halves = acc_columns.reshape(2, block, size)
    mine = jnp.where(band_index == 0, halves[0], halves[1])
    other = jnp.where(band_index == 0, halves[1], halves[0])
    grad = lax.psum_scatter(mine + swapped(other, "tile", 0), "cuts",
                            scatter_dimension=0, tiled=True)
    padded = lax.dynamic_update_slice_in_dim(
        jnp.zeros((wsize, size), jnp.float32), acc_window, band_index * rows, 0)
    small = jnp.concatenate([padded, acc_core, jnp.stack(diags, 0)], 0)
    window, core_total, diag = small_sums(n, -coef * small, wsize, size, months)
    return -coef * grad, window, core_total, diag


def body(trade, factor, scales, core):
    n, tiles = lax.axis_size("cuts"), lax.axis_size("tile")
    months, wsize, size = trade.shape[0], 2 * trade.shape[2], factor.shape[1]
    if factor.shape[0] % 256 or factor.shape[0] < wsize or n < 2 or months > 8:
        return plain(trade, factor, scales, core)
    if wsize % (8 * n * tiles) or size % (8 * n * tiles):
        return plain(trade, factor, scales, core)
    return fused(n, tiles, trade, factor, scales, core)


def solution(mesh):
    return jax.shard_map(
        body,
        mesh=mesh,
        in_specs=(
            P(("groups", "cuts"), "tile", None, None),
            P(("groups", "tile", "cuts"), None),
            P(("groups", "cuts"), None),
            P("groups", None),
        ),
        out_specs=(
            P(("groups", "tile", "cuts"), None),
            P(("groups", "cuts"), None),
            P("groups", None),
            P(("groups", "cuts"), None),
        ),
        check_vma=False,
    )
```
